128 devices in a mesh: prow: 8 (over x, core), pcol: 16 (over y, z).
Axes of the slice: x: 4, y: 4, z: 4, core: 2. Of those that a mesh axis runs over, the one named last changes fastest.
Arguments:
- children: bfloat16 [131072, 6144], P(('prow', 'pcol')), may hold values from -6 to 6
- row_owner: int32 [1024, 1], P(('prow', 'pcol')), may hold values from 0 to 7; in each aligned block of 8 rows (0 to 7, 8 to 15, ...) at most 2 rows name the same one
- row_local: int32 [1024], P(('prow', 'pcol')), may hold values from 0 to 87
- row_within: int32 [1024, 128], P(('prow', 'pcol')), may hold values from 0 to 127, each once within a row
- column_tile: int32 [2, 48], replicated, may hold values from 0 to 63, as said below
- column_within: int32 [2, 48, 128], replicated, may hold values from 0 to 127, each once within a row
- pivot_rows: int32 [128], replicated, may hold values from 0 to 90111, as said below
- lower_inverse: bfloat16 [128, 128], replicated, as said below
- upper_inverse: bfloat16 [128, 128], replicated, as said below
Outputs:
- updated: bfloat16 [90112, 8192], P('prow', 'pcol')
The draws below stay inside these ranges and needn't reach their ends.
Inputs may be any that keep to these rules, and one draw needn't show every extreme that they name: `row_owner`: among the 8 entries of one device no value appears more than 2 times, and on some device one value appears exactly 2 times. `row_within`: each row of 128 entries is a permutation of 0 to 127. `column_tile`: each row names 48 different slab tiles, and in each row all 4 tiles q * 4 to (q + 1) * 4 - 1 of some index q of pcol are named. `column_within`: each last-dimension row is a permutation of 0 to 127. `pivot_rows`: 128 different front rows. `lower_inverse`: zero above the diagonal, positive diagonal. `upper_inverse`: zero below the diagonal, positive diagonal.
All inputs are finite; a program needn't handle non-finite values.
Results may differ from the reference program's by a relative error of at most 0.0065.
Values may be sent and summed in bfloat16 or wider, within the bound.
No kernel may reach another device: no remote copies, remote signals or barrier semaphores. Data moves between devices by JAX's collectives and lax.ppermute only.
A program may use at most 320 MiB of HBM per device.

```python
import math
import jax
import jax.numpy as jnp
import numpy as np
from jax import lax

TILE = 128
FRONT = 90112
SLAB = 8192
CHILD_COLS = 6144
TILES_DEV = 8
ROW_CAP = 2
CHILD_TILES = 1024
MT_DEV = 88
ST_DEV = 4
SLAB_TILES = 64
CHILD_COL_TILES = 48
N_PROW = 8
N_PCOL = 16


def draw_column_tile(key, part):
    key = jax.random.fold_in(key, 11)
    others = SLAB_TILES - ST_DEV
    chosen = []
    for child_id in range(2):
        child_key = jax.random.fold_in(key, child_id)
        owner_key, pick_key, mix_key = jax.random.split(child_key, 3)
        full_owner = jax.random.randint(owner_key, (), 0, SLAB_TILES // ST_DEV)
        shuffled = jax.random.permutation(pick_key, others)[:CHILD_COL_TILES - ST_DEV]
        spare_tiles = (full_owner * ST_DEV + ST_DEV + shuffled) % SLAB_TILES
        owner_tiles = full_owner * ST_DEV + jnp.arange(ST_DEV)
        picked = jnp.concatenate([owner_tiles, spare_tiles]).astype(jnp.int32)
        chosen.append(jax.random.permutation(mix_key, picked))
    return jnp.stack(chosen).astype(jnp.int32)


def draw_pivot_rows(key, part):
    key = jax.random.fold_in(key, 23)
    return jax.random.permutation(key, FRONT)[:TILE].astype(jnp.int32)


def triangle(key, strict_mask):
    spread_key, diagonal_key = jax.random.split(key)
    spread_part = 0.04 * jax.random.normal(spread_key, (TILE, TILE), jnp.float32)
    diagonal = jax.random.uniform(diagonal_key, (TILE,), jnp.float32, 0.15, 0.3)
    return (jnp.where(strict_mask, spread_part, 0.0) + jnp.diag(diagonal)).astype(jnp.bfloat16)


def draw_lower_inverse(key, part):
    key = jax.random.fold_in(key, 31)
    index_grid = jnp.arange(TILE)
    return triangle(key, index_grid[:, None] > index_grid[None, :])


def draw_upper_inverse(key, part):
    key = jax.random.fold_in(key, 37)
    index_grid = jnp.arange(TILE)
    return triangle(key, index_grid[:, None] < index_grid[None, :])


def with_ends(array, key, least, high):
    spot = [jax.random.randint(jax.random.fold_in(key, axis), (), 0, length) for axis, length in enumerate(array.shape)]
    widest = array.shape.index(max(array.shape))
    next_to = spot[:widest] + [(spot[widest] + 1) % array.shape[widest]] + spot[widest + 1:]
    return array.at[tuple(spot)].set(least).at[tuple(next_to)].set(high)


def level_of(key, shape, cuts, smallest, top_value):
    gain, own = 1.0, jax.random.fold_in(key, 6)
    for position, shards_of in cuts:
        steps = jnp.exp(jax.random.uniform(jax.random.fold_in(own, position), (shards_of,), jnp.float32, smallest / len(cuts), top_value / len(cuts)))
        gain = gain * jnp.repeat(steps, shape[position] // shards_of).reshape([-1 if axis == position else 1 for axis in range(len(shape))])
    return gain


def deal_out(key, own, number, rows, count, top, most, lean):
    order = jax.random.permutation(key, count)
    heavy_load, common = load_shares(count, rows * top, most, lean, True), load_shares(count, rows * top, most, lean, False)
    places = jnp.arange(count)

    def named(lengths, rotation):
        used = int((lengths > 0).sum())
        fixed = max(1, used // 4)
        moved = fixed + (places - fixed + rotation * (used - fixed)) % max(1, count - fixed)
        return jnp.zeros((count,), jnp.int32).at[order[jnp.where(places < fixed, places, moved)]].set(jnp.asarray(lengths, jnp.int32))

    lengths = jnp.where(number % 4 == 0, named(heavy_load, number // 4), named(common, number - number // 4 - 1))
    mixed = jax.random.permutation(jax.random.fold_in(own, 3), count)
    giver, sink = mixed[0:count // 2 * 2:2], mixed[1:count // 2 * 2:2]
    room = jnp.minimum(lengths[giver] - 1, most - lengths[sink]) // 2
    room = jnp.where((giver == order[0]) | (sink == order[0]) | (lengths[sink] == 0), 0, jnp.maximum(room, 0))
    moved = jax.random.randint(jax.random.fold_in(own, 4), (count // 2,), 0, 1 << 20) % (room + 1)
    lengths = lengths.at[giver].add(-moved).at[sink].add(moved)
    labels = jnp.searchsorted(jnp.cumsum(lengths), jnp.arange(rows * top), side="right").astype(jnp.int32)
    listing = labels.reshape(top, rows).T
    listing = listing[jax.random.permutation(jax.random.fold_in(own, 1), rows)]
    rotation = jax.random.randint(jax.random.fold_in(own, 2), (rows, 1), 0, top)
    return jnp.take_along_axis(listing, (jnp.arange(top)[None, :] + rotation) % top, axis=1)


def load_shares(number_of, total, most, lean, full):
    weights = [(1 << 20) // math.isqrt(grade ** lean) + 1 for grade in range(1, number_of + 1)]
    largest = most if full else min(most, max(-(-total // number_of), total * weights[0] // sum(weights)))
    least = 1 if total - largest >= number_of - 1 else 0
    counts, surplus = [largest] + [least] * (number_of - 1), total - largest - least * (number_of - 1)
    while surplus > 0:
        free = [i for i in range(1, number_of) if counts[i] < largest] or [i for i in range(1, number_of) if counts[i] < most]
        whole, remaining = sum([weights[i] for i in free]), surplus
        for i in free:
            extra = min(most - counts[i], max(1, remaining * weights[i] // whole), surplus)
            counts[i] = counts[i] + extra
            surplus = surplus - extra
    return np.array(counts)


def scatter_about(own_key, extent, spread, most, cuts=(), kind=jnp.bfloat16):
    factor_of = level_of(own_key, extent, cuts, -0.22, 0.18) if cuts else 1.0
    drawn = jax.random.normal(own_key, extent, jnp.float32) * spread * factor_of
    return jnp.minimum(jnp.maximum(drawn, -most), most).astype(kind)


def setup_inputs(seed: int = 0) -> dict:
    streams_of = jax.random.split(jax.random.key(seed), 10)
    children = scatter_about(streams_of[0], (CHILD_TILES * TILE, CHILD_COLS), 1.0, 6.0, ((0, 128),))
    row_owner_keys = jax.random.split(jax.random.fold_in(streams_of[1], 1), CHILD_TILES // TILES_DEV)
    row_owner_turns = jax.random.permutation(jax.random.fold_in(streams_of[1], 3), CHILD_TILES // TILES_DEV)
    row_owner = jax.vmap(lambda own, number: deal_out(jax.random.fold_in(streams_of[1], 2), own, number, TILES_DEV, N_PROW, 1, ROW_CAP, 2))(row_owner_keys, row_owner_turns).reshape((CHILD_TILES, 1))
    row_local = with_ends(jax.random.randint(streams_of[2], (CHILD_TILES,), 0, MT_DEV), jax.random.fold_in(streams_of[2], 1), 0, MT_DEV - 1).astype(jnp.int32)
    row_within = jax.vmap(lambda own: jax.random.permutation(own, TILE))(jax.random.split(streams_of[3], CHILD_TILES)).reshape((CHILD_TILES, TILE)).astype(jnp.int32)
    column_tile = draw_column_tile(jax.random.fold_in(streams_of[9], 71), 0)
    column_within = jax.vmap(lambda own: jax.random.permutation(own, TILE))(jax.random.split(streams_of[5], 2 * CHILD_COL_TILES)).reshape((2, CHILD_COL_TILES, TILE)).astype(jnp.int32)
    pivot_rows = draw_pivot_rows(jax.random.fold_in(streams_of[9], 71), 0)
    lower_inverse = draw_lower_inverse(jax.random.fold_in(streams_of[9], 71), 0)
    upper_inverse = draw_upper_inverse(jax.random.fold_in(streams_of[9], 71), 0)
    return {"children": children, "row_owner": row_owner, "row_local": row_local, "row_within": row_within, "column_tile": column_tile, "column_within": column_within, "pivot_rows": pivot_rows, "lower_inverse": lower_inverse, "upper_inverse": upper_inverse}


def reference(children, row_owner, row_local, row_within, column_tile, column_within, pivot_rows, lower_inverse, upper_inverse):
    tile_size = TILE
    front_tiles = FRONT // (TILE * N_PROW)
    half_rows = children.shape[0] // 2
    parent_tile = row_owner[:, 0] * front_tiles + row_local
    row_index = (parent_tile[:, None] * tile_size + row_within).reshape(-1).astype(jnp.int32)
    slab_tiles = SLAB // TILE
    child_col_tiles = CHILD_COLS // TILE
    tile_hits = (column_tile[:, :, None] == jnp.arange(slab_tiles, dtype=jnp.int32)[None, None, :]).astype(jnp.int32)
    source_tile = jnp.sum(tile_hits * jnp.arange(child_col_tiles, dtype=jnp.int32)[None, :, None], axis=1)
    present = jnp.sum(tile_hits, axis=1)
    slot_ids = jnp.arange(tile_size, dtype=jnp.int32)
    inverse = jnp.sum((column_within[:, :, :, None] == slot_ids[None, None, None, :]).astype(jnp.int32) * slot_ids[None, None, :, None], axis=2)
    source_col = (inverse[jnp.arange(2, dtype=jnp.int32)[:, None], source_tile] + source_tile[:, :, None] * tile_size).astype(jnp.int32)
    block_tiles = slab_tiles // N_PCOL
    block_width = block_tiles * tile_size

    def assemble(block_id):
        start = (block_id * block_tiles).astype(jnp.int32)
        running_sum = jnp.zeros((FRONT, block_width), jnp.float32)
        for child_id in range(2):
            col_index = lax.dynamic_slice_in_dim(source_col[child_id], start, block_tiles, 0).reshape(-1)
            keep_cols = jnp.repeat(lax.dynamic_slice_in_dim(present[child_id], start, block_tiles, 0), tile_size)
            child_rows = children[child_id * half_rows:(child_id + 1) * half_rows]
            taken = jnp.take(child_rows, col_index, axis=1).astype(jnp.float32) * keep_cols[None, :].astype(jnp.float32)
            running_sum = running_sum.at[row_index[child_id * half_rows:(child_id + 1) * half_rows]].add(taken)
        return running_sum.astype(jnp.bfloat16)

    first_block = assemble(jnp.int32(0))
    lower_panel = jnp.dot(first_block[:, :tile_size], upper_inverse, preferred_element_type=jnp.float32).astype(jnp.bfloat16)

    def update(block_id, result_slab):
        block_id = jnp.asarray(block_id).astype(jnp.int32)
        front_block = assemble(block_id)
        pivot_block = jnp.take(front_block, pivot_rows, axis=0)
        upper_rows = jnp.dot(lower_inverse, pivot_block, preferred_element_type=jnp.float32).astype(jnp.bfloat16)
        schur_part = (front_block.astype(jnp.float32) - jnp.dot(lower_panel, upper_rows, preferred_element_type=jnp.float32)).astype(jnp.bfloat16)
        schur_part = schur_part.at[pivot_rows].set(upper_rows)
        return lax.dynamic_update_slice_in_dim(result_slab, schur_part, (block_id * block_width).astype(jnp.int32), 1)

    updated = lax.fori_loop(0, N_PCOL, update, jnp.zeros((FRONT, SLAB), jnp.bfloat16))
    return updated.at[:, :tile_size].set(lower_panel)
```

```python
import functools

import jax
import jax.numpy as jnp
from jax import lax
from jax.experimental import pallas as pl
from jax.experimental.pallas import tpu as pltpu
from jax.sharding import PartitionSpec as P

TILE = 128
FRONT = 90112
SLAB = 8192
N_PROW = 8
N_PCOL = 16
N_DEV = N_PROW * N_PCOL
FRONT_TILES = FRONT // TILE // N_PROW
LOCAL_ROWS = FRONT_TILES * TILE
SLOTS = SLAB // TILE // N_PCOL
OWN_TILES = 8
RANKS = 2
CHUNKS = ((0, 1), (1, 1), (2, 2))
GROUP = 8
ROW_BLOCK = 704
MIB = 1 << 20


def one_hot_t(index_row):
    slot = lax.broadcasted_iota(jnp.int32, (TILE, TILE), 0)
    return jnp.where(slot == index_row, 1.0, 0.0).astype(jnp.bfloat16)


def pack_kernel(first, src, present, owner, rank, x_ref, cw_ref, rw_ref, out_ref, perm):
    group, slot = pl.program_id(0), pl.program_id(1)

    @pl.when((group == 0) & (slot == 0))
    def _():
        for t in range(OWN_TILES):
            perm[t] = one_hot_t(rw_ref[t : t + 1, :])

    here = present[group * SLOTS + first + slot]

    @pl.when(here == 0)
    def _():
        out_ref[...] = jnp.zeros_like(out_ref)

    @pl.when(here != 0)
    def _():
        moved = lax.dot_general(
            x_ref[...],
            one_hot_t(cw_ref[0]),
            (((1,), (1,)), ((), ())),
            preferred_element_type=jnp.float32,
        ).astype(jnp.bfloat16)
        for t in range(OWN_TILES):
            tile = jnp.dot(
                perm[t], moved[t * TILE : (t + 1) * TILE], preferred_element_type=jnp.float32
            )
            out_ref[owner[t], 0, rank[t], 0] = tile.astype(jnp.bfloat16)


def pack(first, width, src, present, owner, rank, children, col_within, row_within):
    def source(q, s, src, present, owner, rank):
        return src[q * SLOTS + first + s]

    return pl.pallas_call(
        functools.partial(pack_kernel, first),
        out_shape=jax.ShapeDtypeStruct(
            (N_PROW, N_PCOL, RANKS, width, TILE, TILE), jnp.bfloat16
        ),
        grid_spec=pltpu.PrefetchScalarGridSpec(
            num_scalar_prefetch=4,
            grid=(N_PCOL, width),
            in_specs=[
                pl.BlockSpec((OWN_TILES * TILE, TILE), lambda *a: (0, source(*a))),
                pl.BlockSpec((1, 1, TILE), lambda *a: (source(*a), 0, 0)),
                pl.BlockSpec((OWN_TILES, TILE), lambda *a: (0, 0)),
            ],
            out_specs=pl.BlockSpec(
                (N_PROW, 1, RANKS, 1, TILE, TILE), lambda q, s, *a: (0, q, 0, s, 0, 0)
            ),
            scratch_shapes=[pltpu.VMEM((OWN_TILES, TILE, TILE), jnp.bfloat16)],
        ),
        compiler_params=pltpu.CompilerParams(vmem_limit_bytes=24 * MIB),
        cost_estimate=pl.CostEstimate(
            flops=4 * N_PCOL * width * OWN_TILES * TILE**3,
            bytes_accessed=3 * N_PCOL * width * OWN_TILES * TILE * TILE * 2,
            transcendentals=0,
        ),
    )(src, present, owner, rank, children, col_within, row_within)


def accumulate_kernel(width, bins, pivots, x_ref, front_ref, pivot_ref, acc, picked):
    step = pl.program_id(0)
    cols = width * TILE

    @pl.when(step == 0)
    def _():
        @pl.loop(0, FRONT_TILES)
        def _(i):
            acc[pl.ds(pl.multiple_of(i * TILE, TILE), TILE), :] = jnp.zeros(
                (TILE, cols), jnp.float32
            )

    @pl.loop(0, GROUP)
    def _(g):
        for r in range(RANKS):
            place = bins[(step * GROUP + g) * RANKS + r]

            @pl.when(place >= 0)
            def _():
                rows = pl.ds(pl.multiple_of(place * TILE, TILE), TILE)
                for c in range(width):
                    acc[rows, c * TILE : (c + 1) * TILE] += x_ref[g, r, c].astype(
                        jnp.float32
                    )

    @pl.when(step == pl.num_programs(0) - 1)
    def _():
        @pl.loop(0, FRONT_TILES)
        def _(i):
            rows = pl.ds(pl.multiple_of(i * TILE, TILE), TILE)
            front_ref[rows, :] = acc[rows, :].astype(jnp.bfloat16)

        @pl.loop(0, TILE)
        def _(j):
            row = pivots[j]
            mine = (row >= 0).astype(jnp.float32)
            value = acc[pl.ds(jnp.maximum(row, 0), 1), :]
            picked[pl.ds(j, 1), :] = value * mine

        pivot_ref[...] = picked[...].astype(jnp.bfloat16)


def accumulate(width, bins, pivots, arrived):
    cols = width * TILE
    return pl.pallas_call(
        functools.partial(accumulate_kernel, width),
        out_shape=[
            jax.ShapeDtypeStruct((LOCAL_ROWS, cols), jnp.bfloat16),
            jax.ShapeDtypeStruct((TILE, cols), jnp.bfloat16),
        ],
        grid_spec=pltpu.PrefetchScalarGridSpec(
            num_scalar_prefetch=2,
            grid=(N_DEV // GROUP,),
            in_specs=[
                pl.BlockSpec((GROUP, RANKS, width, TILE, TILE), lambda i, *a: (i, 0, 0, 0, 0))
            ],
            out_specs=[
                pl.BlockSpec((LOCAL_ROWS, cols), lambda i, *a: (0, 0)),
                pl.BlockSpec((TILE, cols), lambda i, *a: (0, 0)),
            ],
            scratch_shapes=[
                pltpu.VMEM((LOCAL_ROWS, cols), jnp.float32),
                pltpu.VMEM((TILE, cols), jnp.float32),
            ],
        ),
        compiler_params=pltpu.CompilerParams(vmem_limit_bytes=48 * MIB),
        cost_estimate=pl.CostEstimate(
            flops=N_DEV * RANKS * TILE * cols,
            bytes_accessed=(N_DEV * RANKS * TILE + LOCAL_ROWS) * cols * 2,
            transcendentals=0,
        ),
    )(bins, pivots, arrived)


def update_kernel(n_chunks, is_first, *refs):
    fronts, (panel_ref, pivot_ref, row_ref, linv_ref, uinv_ref, out_ref, upper) = (
        refs[:n_chunks],
        refs[n_chunks:],
    )
    step = pl.program_id(0)

    @pl.when(step == 0)
    def _():
        block = pivot_ref[0].astype(jnp.float32)
        for p in range(1, N_PROW):
            block = block + pivot_ref[p].astype(jnp.float32)
        upper[...] = jnp.dot(
            linv_ref[...], block.astype(jnp.bfloat16), preferred_element_type=jnp.float32
        ).astype(jnp.bfloat16)

    lower = (
        jnp.dot(panel_ref[...], uinv_ref[...], preferred_element_type=jnp.float32)
        .astype(jnp.bfloat16)
        .astype(jnp.float32)
    )
    rows = lax.broadcasted_iota(jnp.int32, (ROW_BLOCK, TILE), 0) + step * ROW_BLOCK
    chosen = jnp.where(rows == row_ref[...], 1.0, 0.0)
    replaced = jnp.max(chosen, axis=1, keepdims=True)
    kept = 1.0 - replaced
    factor = jnp.where(replaced > 0.0, chosen, -lower).astype(jnp.bfloat16)
    at = 0
    for k in range(n_chunks):
        cols = fronts[k].shape[1]
        product = jnp.dot(
            factor, upper[:, at : at + cols], preferred_element_type=jnp.float32
        )
        result = jnp.where(replaced > 0.0, product, fronts[k][...].astype(jnp.float32) + product)
        out_ref[:, at : at + cols] = result.astype(jnp.bfloat16)
        at += cols

    @pl.when(is_first[0] != 0)
    def _():
        out_ref[:, 0:TILE] = lower.astype(jnp.bfloat16)


def update(is_first, fronts, panel, pivots, rows, linv, uinv):
    cols = SLOTS * TILE
    whole = lambda *shape: pl.BlockSpec(shape, lambda i, *a: (0,) * len(shape))
    return pl.pallas_call(
        functools.partial(update_kernel, len(fronts)),
        out_shape=jax.ShapeDtypeStruct((LOCAL_ROWS, cols), jnp.bfloat16),
        grid_spec=pltpu.PrefetchScalarGridSpec(
            num_scalar_prefetch=1,
            grid=(LOCAL_ROWS // ROW_BLOCK,),
            in_specs=[
                pl.BlockSpec((ROW_BLOCK, f.shape[1]), lambda i, *a: (i, 0)) for f in fronts
            ]
            + [
                pl.BlockSpec((ROW_BLOCK, TILE), lambda i, *a: (i, 0)),
                whole(N_PROW, TILE, cols),
                whole(1, TILE),
                whole(TILE, TILE),
                whole(TILE, TILE),
            ],
            out_specs=pl.BlockSpec((ROW_BLOCK, cols), lambda i, *a: (i, 0)),
            scratch_shapes=[pltpu.VMEM((TILE, cols), jnp.bfloat16)],
        ),
        compiler_params=pltpu.CompilerParams(vmem_limit_bytes=32 * MIB),
        cost_estimate=pl.CostEstimate(
            flops=2 * LOCAL_ROWS * TILE * (cols + TILE),
            bytes_accessed=2 * LOCAL_ROWS * cols * 2,
            transcendentals=0,
        ),
    )(is_first, *fronts, panel, pivots, rows, linv, uinv)


def spread_panel(panel, my_pcol):
    pieces = panel.reshape(N_PCOL, LOCAL_ROWS // N_PCOL, TILE)
    piece = pieces[0]
    for q in range(1, N_PCOL):
        got = lax.ppermute(pieces[q], "pcol", [(0, q)])
        piece = jnp.where(my_pcol == q, got, piece)
    whole = jnp.zeros_like(pieces)
    whole = lax.dynamic_update_index_in_dim(whole, piece, my_pcol, 0)
    for i in range(1, N_PCOL):
        got = lax.ppermute(piece, "pcol", [(q, q ^ i) for q in range(N_PCOL)])
        whole = lax.dynamic_update_index_in_dim(whole, got, my_pcol ^ i, 0)
    return whole.reshape(LOCAL_ROWS, TILE)


def on_device(
    children,
    row_owner,
    row_local,
    row_within,
    column_tile,
    column_within,
    pivot_rows,
    lower_inverse,
    upper_inverse,
):
    my_prow = lax.axis_index("prow")
    my_pcol = lax.axis_index("pcol")
    child = my_prow // (N_PROW // 2)
    col_tile = jnp.take(column_tile, child, axis=0)
    col_within = jnp.take(column_within, child, axis=0)
    n_src = col_tile.shape[0]
    hits = (col_tile[:, None] == jnp.arange(SLAB // TILE, dtype=jnp.int32)[None, :]).astype(
        jnp.int32
    )
    src = jnp.sum(hits * jnp.arange(n_src, dtype=jnp.int32)[:, None], axis=0)
    present = jnp.sum(hits, axis=0)
    order = jnp.arange(OWN_TILES, dtype=jnp.int32)
    earlier = order[None, :] < order[:, None]
    owners = row_owner[:, 0]
    rank = jnp.sum(((owners[:, None] == owners[None, :]) & earlier).astype(jnp.int32), axis=1)

    codes = jnp.pad(
        (owners * FRONT_TILES + row_local)[None, :], ((0, 0), (0, TILE - OWN_TILES))
    )
    codes = lax.all_to_all(
        jnp.broadcast_to(codes[None], (N_DEV, 8, TILE)),
        ("prow", "pcol"),
        split_axis=0,
        concat_axis=0,
        tiled=True,
    )[:, 0, :OWN_TILES]
    mine = codes // FRONT_TILES == my_prow
    nth = jnp.sum((mine[:, None, :] & earlier[None]).astype(jnp.int32), axis=2)
    want = jnp.arange(RANKS, dtype=jnp.int32)[None, :, None]
    is_it = mine[:, None, :] & (nth[:, None, :] == want)
    bins = jnp.max(
        jnp.where(is_it, (codes % FRONT_TILES)[:, None, :], -1), axis=2
    ).reshape(-1)

    pivot_local = jnp.where(
        pivot_rows // LOCAL_ROWS == my_prow, pivot_rows % LOCAL_ROWS, -1
    ).astype(jnp.int32)

    fronts, picks = [], []
    panel = None
    for first, width in CHUNKS:
        sent = pack(
            first,
            width,
            src,
            present,
            owners,
            rank,
            children,
            col_within.reshape(n_src, 1, TILE),
            row_within,
        )
        arrived = lax.all_to_all(
            sent.reshape(N_DEV, RANKS, width, TILE, TILE),
            ("prow", "pcol"),
            split_axis=0,
            concat_axis=0,
            tiled=True,
        )
        front, picked = accumulate(width, bins, pivot_local, arrived)
        fronts.append(front)
        picks.append(picked)
        if first == 0:
            panel = spread_panel(front[:, :TILE], my_pcol)
    picked = jnp.concatenate(picks, axis=1)
    pivots = lax.all_to_all(
        jnp.broadcast_to(picked[None], (N_PROW,) + picked.shape),
        "prow",
        split_axis=0,
        concat_axis=0,
        tiled=True,
    )
    return update(
        (my_pcol == 0).astype(jnp.int32).reshape(1),
        fronts,
        panel,
        pivots,
        pivot_local.reshape(1, TILE),
        lower_inverse,
        upper_inverse,
    )


def solution(mesh):
    placed = (
        P(("prow", "pcol"), None),
        P(("prow", "pcol"), None),
        P(("prow", "pcol")),
        P(("prow", "pcol"), None),
        P(),
        P(),
        P(),
        P(),
        P(),
    )
    return jax.shard_map(
        on_device, mesh=mesh, in_specs=placed, out_specs=P("prow", "pcol"), check_vma=False
    )
```

```python
import functools

import jax
import jax.numpy as jnp
from jax import lax
from jax.experimental import pallas as pl
from jax.experimental.pallas import tpu as pltpu
from jax.sharding import PartitionSpec as P

TILE = 128
FRONT = 90112
SLAB = 8192
N_PROW = 8
N_PCOL = 16
N_DEV = N_PROW * N_PCOL
FRONT_TILES = FRONT // TILE // N_PROW
LOCAL_ROWS = FRONT_TILES * TILE
SLOTS = SLAB // TILE // N_PCOL
OWN_TILES = 8
RANKS = 2
WIDE_CHUNKS = ((0, 1), (1, 1), (2, 2))
CHUNKS = ((0, 1), (2, 2), (1, 1))
GROUP = 8
STEPS = 8
ROW_BLOCK = 704
MIB = 1 << 20


def one_hot_t(index_row):
    slot = lax.broadcasted_iota(jnp.int32, (TILE, TILE), 0)
    return jnp.where(slot == index_row, 1.0, 0.0).astype(jnp.bfloat16)


def pack_kernel(first, ranks, src, present, owner, rank, x_ref, cw_ref, rw_ref, out_ref, perm):
    group, slot = pl.program_id(0), pl.program_id(1)

    @pl.when((group == 0) & (slot == 0))
    def _():
        for t in range(OWN_TILES):
            perm[t] = one_hot_t(rw_ref[t : t + 1, :])

    here = present[group * SLOTS + first + slot]

    @pl.when(here == 0)
    def _():
        out_ref[...] = jnp.zeros_like(out_ref)

    @pl.when(here != 0)
    def _():
        moved = lax.dot_general(
            x_ref[...],
            one_hot_t(cw_ref[0]),
            (((1,), (1,)), ((), ())),
            preferred_element_type=jnp.float32,
        ).astype(jnp.bfloat16)
        for t in range(OWN_TILES):
            tile = jnp.dot(
                perm[t], moved[t * TILE : (t + 1) * TILE], preferred_element_type=jnp.float32
            )
            if ranks == RANKS:
                out_ref[owner[t], 0, rank[t], 0] = tile.astype(jnp.bfloat16)
            else:

                @pl.when(rank[t] == 0)
                def _():
                    out_ref[owner[t], 0, 0, 0] = tile.astype(jnp.bfloat16)


def pack(first, width, ranks, src, present, owner, rank, children, col_within, row_within):
    def source(q, s, src, present, owner, rank):
        return src[q * SLOTS + first + s]

    return pl.pallas_call(
        functools.partial(pack_kernel, first, ranks),
        out_shape=jax.ShapeDtypeStruct(
            (N_PROW, N_PCOL, ranks, width, TILE, TILE), jnp.bfloat16
        ),
        grid_spec=pltpu.PrefetchScalarGridSpec(
            num_scalar_prefetch=4,
            grid=(N_PCOL, width),
            in_specs=[
                pl.BlockSpec((OWN_TILES * TILE, TILE), lambda *a: (0, source(*a))),
                pl.BlockSpec((1, 1, TILE), lambda *a: (source(*a), 0, 0)),
                pl.BlockSpec((OWN_TILES, TILE), lambda *a: (0, 0)),
            ],
            out_specs=pl.BlockSpec(
                (N_PROW, 1, ranks, 1, TILE, TILE), lambda q, s, *a: (0, q, 0, s, 0, 0)
            ),
            scratch_shapes=[pltpu.VMEM((OWN_TILES, TILE, TILE), jnp.bfloat16)],
        ),
        compiler_params=pltpu.CompilerParams(vmem_limit_bytes=56 * MIB),
        cost_estimate=pl.CostEstimate(
            flops=4 * N_PCOL * width * OWN_TILES * TILE**3,
            bytes_accessed=3 * N_PCOL * width * OWN_TILES * TILE * TILE * 2,
            transcendentals=0,
        ),
    )(src, present, owner, rank, children, col_within, row_within)


def pack_second_kernel(per_step, src, present, which, x_ref, cw_ref, rw_ref, out_ref):
    perm = one_hot_t(rw_ref[pl.ds(which[0], 1), :])
    for k in range(per_step):
        slot = pl.program_id(0) * per_step + k
        col = src[slot]
        block = x_ref[:, pl.ds(pl.multiple_of(col * TILE, TILE), TILE)]
        moved = lax.dot_general(
            block,
            one_hot_t(cw_ref[pl.ds(col, 1), :]),
            (((1,), (1,)), ((), ())),
            preferred_element_type=jnp.float32,
        ).astype(jnp.bfloat16)
        tile = jnp.dot(perm, moved, preferred_element_type=jnp.float32)
        keep = jnp.full((TILE, TILE), present[slot], jnp.int32) != 0
        out_ref[k] = jnp.where(keep, tile, 0.0).astype(jnp.bfloat16)


def pack_second(src, present, which, children, col_within, row_within):
    n_slots, per_step = SLAB // TILE, 16
    return pl.pallas_call(
        functools.partial(pack_second_kernel, per_step),
        out_shape=jax.ShapeDtypeStruct((n_slots, TILE, TILE), jnp.bfloat16),
        grid_spec=pltpu.PrefetchScalarGridSpec(
            num_scalar_prefetch=3,
            grid=(n_slots // per_step,),
            in_specs=[
                pl.BlockSpec((TILE, children.shape[1]), lambda i, s, p, w: (w[0], 0)),
                pl.BlockSpec(col_within.shape, lambda i, *a: (0, 0)),
                pl.BlockSpec((OWN_TILES, TILE), lambda i, *a: (0, 0)),
            ],
            out_specs=pl.BlockSpec((per_step, TILE, TILE), lambda i, *a: (i, 0, 0)),
        ),
        compiler_params=pltpu.CompilerParams(vmem_limit_bytes=56 * MIB),
        cost_estimate=pl.CostEstimate(
            flops=4 * n_slots * TILE**3,
            bytes_accessed=2 * n_slots * TILE * TILE * 2,
            transcendentals=0,
        ),
    )(src, present, which, children, col_within, row_within)


def sum_kernel(width, counts, bins, seconds, pivots, x_ref, *refs):
    parts, (front_ref, pivot_ref, acc, picked) = refs[: len(counts)], refs[len(counts) :]
    step = pl.program_id(0)
    cols = width * TILE
    per_step = N_DEV // STEPS

    @pl.when(step == 0)
    def _():
        @pl.loop(0, FRONT_TILES)
        def _(i):
            acc[pl.ds(pl.multiple_of(i * TILE, TILE), TILE), :] = jnp.zeros(
                (TILE, cols), jnp.float32
            )

    def add(place, source, index):
        @pl.when(place >= 0)
        def _():
            rows = pl.ds(pl.multiple_of(place * TILE, TILE), TILE)
            for c in range(width):
                acc[rows, c * TILE : (c + 1) * TILE] += source[index, c].astype(jnp.float32)

    for g in range(per_step):
        add(bins[step * per_step + g], x_ref, g)
    at = 0
    for part, count in zip(parts, counts):
        for g in range(count // STEPS):
            add(seconds[at + step * (count // STEPS) + g], part, g)
        at += count

    @pl.when(step == STEPS - 1)
    def _():
        @pl.loop(0, FRONT_TILES)
        def _(i):
            rows = pl.ds(pl.multiple_of(i * TILE, TILE), TILE)
            front_ref[rows, :] = acc[rows, :].astype(jnp.bfloat16)

        @pl.loop(0, TILE)
        def _(j):
            row = pivots[j]
            mine = (row >= 0).astype(jnp.float32)
            value = acc[pl.ds(jnp.maximum(row, 0), 1), :]
            picked[pl.ds(j, 1), :] = value * mine

        pivot_ref[...] = picked[...].astype(jnp.bfloat16)


def sum_chunk(first, width, bins, seconds, pivots, arrived, parts):
    cols = width * TILE
    counts = [p.shape[0] for p in parts]
    return pl.pallas_call(
        functools.partial(sum_kernel, width, counts),
        out_shape=[
            jax.ShapeDtypeStruct((LOCAL_ROWS, cols), jnp.bfloat16),
            jax.ShapeDtypeStruct((TILE, cols), jnp.bfloat16),
        ],
        grid_spec=pltpu.PrefetchScalarGridSpec(
            num_scalar_prefetch=3,
            grid=(STEPS,),
            in_specs=[
                pl.BlockSpec((N_DEV // STEPS, width, TILE, TILE), lambda i, *a: (i, 0, 0, 0))
            ]
            + [
                pl.BlockSpec(
                    (n // STEPS, width, TILE, TILE), lambda i, *a: (i, first // width, 0, 0)
                )
                for n in counts
            ],
            out_specs=[
                pl.BlockSpec((LOCAL_ROWS, cols), lambda i, *a: (0, 0)),
                pl.BlockSpec((TILE, cols), lambda i, *a: (0, 0)),
            ],
            scratch_shapes=[
                pltpu.VMEM((LOCAL_ROWS, cols), jnp.float32),
                pltpu.VMEM((TILE, cols), jnp.float32),
            ],
        ),
        compiler_params=pltpu.CompilerParams(vmem_limit_bytes=56 * MIB),
        cost_estimate=pl.CostEstimate(
            flops=N_DEV * RANKS * TILE * cols,
            bytes_accessed=(N_DEV * RANKS * TILE + LOCAL_ROWS) * cols * 2,
            transcendentals=0,
        ),
    )(bins, seconds, pivots, arrived, *parts)


def accumulate_kernel(width, bins, pivots, x_ref, front_ref, pivot_ref, acc, picked):
    step = pl.program_id(0)
    cols = width * TILE

    @pl.when(step == 0)
    def _():
        @pl.loop(0, FRONT_TILES)
        def _(i):
            acc[pl.ds(pl.multiple_of(i * TILE, TILE), TILE), :] = jnp.zeros(
                (TILE, cols), jnp.float32
            )

    @pl.loop(0, GROUP)
    def _(g):
        for r in range(RANKS):
            place = bins[(step * GROUP + g) * RANKS + r]

            @pl.when(place >= 0)
            def _():
                rows = pl.ds(pl.multiple_of(place * TILE, TILE), TILE)
                for c in range(width):
                    acc[rows, c * TILE : (c + 1) * TILE] += x_ref[g, r, c].astype(
                        jnp.float32
                    )

    @pl.when(step == pl.num_programs(0) - 1)
    def _():
        @pl.loop(0, FRONT_TILES)
        def _(i):
            rows = pl.ds(pl.multiple_of(i * TILE, TILE), TILE)
            front_ref[rows, :] = acc[rows, :].astype(jnp.bfloat16)

        @pl.loop(0, TILE)
        def _(j):
            row = pivots[j]
            mine = (row >= 0).astype(jnp.float32)
            value = acc[pl.ds(jnp.maximum(row, 0), 1), :]
            picked[pl.ds(j, 1), :] = value * mine

        pivot_ref[...] = picked[...].astype(jnp.bfloat16)


def accumulate(width, bins, pivots, arrived):
    cols = width * TILE
    return pl.pallas_call(
        functools.partial(accumulate_kernel, width),
        out_shape=[
            jax.ShapeDtypeStruct((LOCAL_ROWS, cols), jnp.bfloat16),
            jax.ShapeDtypeStruct((TILE, cols), jnp.bfloat16),
        ],
        grid_spec=pltpu.PrefetchScalarGridSpec(
            num_scalar_prefetch=2,
            grid=(N_DEV // GROUP,),
            in_specs=[
                pl.BlockSpec((GROUP, RANKS, width, TILE, TILE), lambda i, *a: (i, 0, 0, 0, 0))
            ],
            out_specs=[
                pl.BlockSpec((LOCAL_ROWS, cols), lambda i, *a: (0, 0)),
                pl.BlockSpec((TILE, cols), lambda i, *a: (0, 0)),
            ],
            scratch_shapes=[
                pltpu.VMEM((LOCAL_ROWS, cols), jnp.float32),
                pltpu.VMEM((TILE, cols), jnp.float32),
            ],
        ),
        compiler_params=pltpu.CompilerParams(vmem_limit_bytes=56 * MIB),
        cost_estimate=pl.CostEstimate(
            flops=N_DEV * RANKS * TILE * cols,
            bytes_accessed=(N_DEV * RANKS * TILE + LOCAL_ROWS) * cols * 2,
            transcendentals=0,
        ),
    )(bins, pivots, arrived)


def update_kernel(n_chunks, is_first, *refs):
    fronts, (panel_ref, pivot_ref, row_ref, linv_ref, uinv_ref, out_ref, upper) = (
        refs[:n_chunks],
        refs[n_chunks:],
    )
    step = pl.program_id(0)

    @pl.when(step == 0)
    def _():
        block = pivot_ref[0].astype(jnp.float32)
        for p in range(1, pivot_ref.shape[0]):
            block = block + pivot_ref[p].astype(jnp.float32)
        upper[...] = jnp.dot(
            linv_ref[...], block.astype(jnp.bfloat16), preferred_element_type=jnp.float32
        ).astype(jnp.bfloat16)

    lower = (
        jnp.dot(panel_ref[...], uinv_ref[...], preferred_element_type=jnp.float32)
        .astype(jnp.bfloat16)
        .astype(jnp.float32)
    )
    rows = lax.broadcasted_iota(jnp.int32, (ROW_BLOCK, TILE), 0) + step * ROW_BLOCK
    chosen = jnp.where(rows == row_ref[...], 1.0, 0.0)
    replaced = jnp.max(chosen, axis=1, keepdims=True)
    kept = 1.0 - replaced
    factor = jnp.where(replaced > 0.0, chosen, -lower).astype(jnp.bfloat16)
    at = 0
    for k in range(n_chunks):
        cols = fronts[k].shape[1]
        product = jnp.dot(
            factor, upper[:, at : at + cols], preferred_element_type=jnp.float32
        )
        result = jnp.where(replaced > 0.0, product, fronts[k][...].astype(jnp.float32) + product)
        out_ref[:, at : at + cols] = result.astype(jnp.bfloat16)
        at += cols

    @pl.when(is_first[0] != 0)
    def _():
        out_ref[:, 0:TILE] = lower.astype(jnp.bfloat16)


def update(is_first, fronts, panel, pivots, rows, linv, uinv):
    cols = SLOTS * TILE
    whole = lambda *shape: pl.BlockSpec(shape, lambda i, *a: (0,) * len(shape))
    return pl.pallas_call(
        functools.partial(update_kernel, len(fronts)),
        out_shape=jax.ShapeDtypeStruct((LOCAL_ROWS, cols), jnp.bfloat16),
        grid_spec=pltpu.PrefetchScalarGridSpec(
            num_scalar_prefetch=1,
            grid=(LOCAL_ROWS // ROW_BLOCK,),
            in_specs=[
                pl.BlockSpec((ROW_BLOCK, f.shape[1]), lambda i, *a: (i, 0)) for f in fronts
            ]
            + [
                pl.BlockSpec((ROW_BLOCK, TILE), lambda i, *a: (i, 0)),
                whole(*pivots.shape),
                whole(1, TILE),
                whole(TILE, TILE),
                whole(TILE, TILE),
            ],
            out_specs=pl.BlockSpec((ROW_BLOCK, cols), lambda i, *a: (i, 0)),
            scratch_shapes=[pltpu.VMEM((TILE, cols), jnp.bfloat16)],
        ),
        compiler_params=pltpu.CompilerParams(vmem_limit_bytes=56 * MIB),
        cost_estimate=pl.CostEstimate(
            flops=2 * LOCAL_ROWS * TILE * (cols + TILE),
            bytes_accessed=2 * LOCAL_ROWS * cols * 2,
            transcendentals=0,
        ),
    )(is_first, *fronts, panel, pivots, rows, linv, uinv)


def exchange(parts, axes):
    return lax.all_to_all(parts, axes, split_axis=0, concat_axis=0, tiled=True)


def gather_prow(own):
    def shifted(value, by):
        return lax.ppermute(value, "prow", [(p, (p + 2 * by) % N_PROW) for p in range(N_PROW)])

    half = own.shape[0] // 2
    before, after = shifted(own, 1), shifted(own, -1)
    far_low = shifted(before[:half], 1)
    far_high = shifted(after[half:], -1)
    here = [own, before, after, far_low, far_high]
    there = [lax.ppermute(v, "prow", [(p, p ^ 1) for p in range(N_PROW)]) for v in here]
    named = [(0, 2 * half), (0, 2 * half), (0, 2 * half), (0, half), (half, half)]
    shifts = [0, -1, 1, -2, 2]
    places = [
        (flip, shift, begin, count)
        for flip in (0, 1)
        for shift, (begin, count) in zip(shifts, named)
    ]
    return here + there, places


def spread_panel(panel, my_pcol):
    pieces = panel.reshape(N_PCOL, LOCAL_ROWS // N_PCOL, TILE)
    piece = pieces[0]
    for q in range(1, N_PCOL):
        got = lax.ppermute(pieces[q], "pcol", [(0, q)])
        piece = jnp.where(my_pcol == q, got, piece)
    whole = jnp.zeros_like(pieces)
    whole = lax.dynamic_update_index_in_dim(whole, piece, my_pcol, 0)
    for i in range(1, N_PCOL):
        got = lax.ppermute(piece, "pcol", [(q, q ^ i) for q in range(N_PCOL)])
        whole = lax.dynamic_update_index_in_dim(whole, got, my_pcol ^ i, 0)
    return whole.reshape(LOCAL_ROWS, TILE)


def on_device(
    children,
    row_owner,
    row_local,
    row_within,
    column_tile,
    column_within,
    pivot_rows,
    lower_inverse,
    upper_inverse,
):
    my_prow = lax.axis_index("prow")
    my_pcol = lax.axis_index("pcol")
    child = my_prow // (N_PROW // 2)
    col_tile = jnp.take(column_tile, child, axis=0)
    col_within = jnp.take(column_within, child, axis=0)
    n_src = col_tile.shape[0]
    hits = (col_tile[:, None] == jnp.arange(SLAB // TILE, dtype=jnp.int32)[None, :]).astype(
        jnp.int32
    )
    src = jnp.sum(hits * jnp.arange(n_src, dtype=jnp.int32)[:, None], axis=0)
    present = jnp.sum(hits, axis=0)
    order = jnp.arange(OWN_TILES, dtype=jnp.int32)
    earlier = order[None, :] < order[:, None]
    owners = row_owner[:, 0]
    rank = jnp.sum(((owners[:, None] == owners[None, :]) & earlier).astype(jnp.int32), axis=1)

    codes = jnp.pad(
        (owners * FRONT_TILES + row_local)[None, :], ((0, 0), (0, TILE - OWN_TILES))
    )
    codes = lax.all_to_all(
        jnp.broadcast_to(codes[None], (N_DEV, 8, TILE)),
        ("prow", "pcol"),
        split_axis=0,
        concat_axis=0,
        tiled=True,
    )[:, 0, :OWN_TILES]
    mine = codes // FRONT_TILES == my_prow
    nth = jnp.sum((mine[:, None, :] & earlier[None]).astype(jnp.int32), axis=2)
    want = jnp.arange(RANKS, dtype=jnp.int32)[None, :, None]
    is_it = mine[:, None, :] & (nth[:, None, :] == want)
    bins = jnp.max(jnp.where(is_it, (codes % FRONT_TILES)[:, None, :], -1), axis=2)

    second = rank == 1
    which = jnp.min(jnp.where(second, order, OWN_TILES - 1)).reshape(1)
    owner_of = codes // FRONT_TILES
    again = jnp.sum(
        ((owner_of[:, :, None] == owner_of[:, None, :]) & earlier[None]).astype(jnp.int32), axis=2
    )
    is_second = again == 1
    more = jnp.max(jnp.sum(is_second.astype(jnp.int32), axis=1)) > 1
    seconds = jnp.max(
        jnp.where(is_second & mine, codes % FRONT_TILES, -1), axis=1
    ).reshape(N_PROW, N_PCOL)

    pivot_local = jnp.where(
        pivot_rows // LOCAL_ROWS == my_prow, pivot_rows % LOCAL_ROWS, -1
    ).astype(jnp.int32)
    is_first = (my_pcol == 0).astype(jnp.int32).reshape(1)
    pivot_line = pivot_local.reshape(1, TILE)
    col_line = col_within.reshape(n_src, 1, TILE)

    sent = pack_second(src, present, which, children, col_within, row_within)
    own = exchange(sent.reshape(N_PCOL, SLOTS, TILE, TILE), "pcol")
    parts, places = gather_prow(own)
    places = jnp.concatenate(
        [
            jnp.take(seconds, ((my_prow ^ flip) + 2 * shift) % N_PROW, axis=0)[
                begin : begin + count
            ]
            for flip, shift, begin, count in places
        ]
    )

    fronts, picks = {}, {}
    panel = None
    for first, width in CHUNKS:
        sent = pack(
            first, width, 1, src, present, owners, rank, children, col_line, row_within
        )
        arrived = exchange(sent.reshape(N_DEV, width, TILE, TILE), ("prow", "pcol"))
        fronts[first], picks[first] = sum_chunk(
            first, width, bins[:, 0], places, pivot_local, arrived, parts
        )
        if first == 0:
            panel = spread_panel(fronts[first][:, :TILE], my_pcol)
    fronts = [fronts[k] for k in sorted(fronts)]
    pivots = jnp.concatenate([picks[k] for k in sorted(picks)], axis=1)
    for bit in (1, 2):
        pivots = pivots + lax.ppermute(pivots, "prow", [(p, p ^ bit) for p in range(N_PROW)])
    pivots = jnp.stack(
        [pivots, lax.ppermute(pivots, "prow", [(p, p ^ 4) for p in range(N_PROW)])]
    )

    def narrow():
        return update(
            is_first, fronts, panel, pivots, pivot_line, lower_inverse, upper_inverse
        )

    def wide():
        fronts, picks = [], []
        for first, width in WIDE_CHUNKS:
            sent = pack(
                first, width, RANKS, src, present, owners, rank, children, col_line, row_within
            )
            arrived = exchange(
                sent.reshape(N_DEV, RANKS, width, TILE, TILE), ("prow", "pcol")
            )
            front, picked = accumulate(width, bins.reshape(-1), pivot_local, arrived)
            fronts.append(front)
            picks.append(picked)
        panel = spread_panel(fronts[0][:, :TILE], my_pcol)
        picked = jnp.concatenate(picks, axis=1)
        pivots = exchange(jnp.broadcast_to(picked[None], (N_PROW,) + picked.shape), "prow")
        return update(
            is_first, fronts, panel, pivots, pivot_line, lower_inverse, upper_inverse
        )

    return lax.cond(more, wide, narrow)


def solution(mesh):
    placed = (
        P(("prow", "pcol"), None),
        P(("prow", "pcol"), None),
        P(("prow", "pcol")),
        P(("prow", "pcol"), None),
        P(),
        P(),
        P(),
        P(),
        P(),
    )
    return jax.shard_map(
        on_device, mesh=mesh, in_specs=placed, out_specs=P("prow", "pcol"), check_vma=False
    )
```

```python
import functools

import jax
import jax.numpy as jnp
from jax import lax
from jax.experimental import pallas as pl
from jax.experimental.pallas import tpu as pltpu
from jax.sharding import PartitionSpec as P

TILE = 128
FRONT = 90112
SLAB = 8192
N_PROW = 8
N_PCOL = 16
N_DEV = N_PROW * N_PCOL
FRONT_TILES = FRONT // TILE // N_PROW
LOCAL_ROWS = FRONT_TILES * TILE
SLOTS = SLAB // TILE // N_PCOL
OWN_TILES = 8
RANKS = 2
WIDE_CHUNKS = ((0, 1), (1, 1), (2, 2))
CHUNKS = ((0, 1), (2, 2), (1, 1))
GROUP = 8
STEPS = 8
ROW_BLOCK = 704
MIB = 1 << 20


def one_hot_t(index_row):
    slot = lax.broadcasted_iota(jnp.int32, (TILE, TILE), 0)
    return jnp.where(slot == index_row, 1.0, 0.0).astype(jnp.bfloat16)


def pack_kernel(first, ranks, src, present, owner, rank, x_ref, cw_ref, rw_ref, out_ref, perm):
    group, slot = pl.program_id(0), pl.program_id(1)

    @pl.when((group == 0) & (slot == 0))
    def _():
        for t in range(OWN_TILES):
            perm[t] = one_hot_t(rw_ref[t : t + 1, :])

    here = present[group * SLOTS + first + slot]

    @pl.when(here == 0)
    def _():
        out_ref[...] = jnp.zeros_like(out_ref)

    @pl.when(here != 0)
    def _():
        moved = lax.dot_general(
            x_ref[...],
            one_hot_t(cw_ref[0]),
            (((1,), (1,)), ((), ())),
            preferred_element_type=jnp.float32,
        ).astype(jnp.bfloat16)
        for t in reversed(range(OWN_TILES)):
            tile = jnp.dot(
                perm[t], moved[t * TILE : (t + 1) * TILE], preferred_element_type=jnp.float32
            )
            place = rank[t] if ranks == RANKS else 0
            out_ref[owner[t], 0, place, 0] = tile.astype(jnp.bfloat16)


def pack(first, width, ranks, src, present, owner, rank, children, col_within, row_within):
    def source(q, s, src, present, owner, rank):
        return src[q * SLOTS + first + s]

    return pl.pallas_call(
        functools.partial(pack_kernel, first, ranks),
        out_shape=jax.ShapeDtypeStruct(
            (N_PROW, N_PCOL, ranks, width, TILE, TILE), jnp.bfloat16
        ),
        grid_spec=pltpu.PrefetchScalarGridSpec(
            num_scalar_prefetch=4,
            grid=(N_PCOL, width),
            in_specs=[
                pl.BlockSpec((OWN_TILES * TILE, TILE), lambda *a: (0, source(*a))),
                pl.BlockSpec((1, 1, TILE), lambda *a: (source(*a), 0, 0)),
                pl.BlockSpec((OWN_TILES, TILE), lambda *a: (0, 0)),
            ],
            out_specs=pl.BlockSpec(
                (N_PROW, 1, ranks, 1, TILE, TILE), lambda q, s, *a: (0, q, 0, s, 0, 0)
            ),
            scratch_shapes=[pltpu.VMEM((OWN_TILES, TILE, TILE), jnp.bfloat16)],
        ),
        compiler_params=pltpu.CompilerParams(vmem_limit_bytes=56 * MIB),
        cost_estimate=pl.CostEstimate(
            flops=4 * N_PCOL * width * OWN_TILES * TILE**3,
            bytes_accessed=3 * N_PCOL * width * OWN_TILES * TILE * TILE * 2,
            transcendentals=0,
        ),
    )(src, present, owner, rank, children, col_within, row_within)


def pack_second_kernel(per_step, src, present, which, x_ref, cw_ref, rw_ref, out_ref):
    perm = one_hot_t(rw_ref[pl.ds(which[0], 1), :])
    for k in range(per_step):
        slot = pl.program_id(0) * per_step + k
        col = src[slot]
        block = x_ref[:, pl.ds(pl.multiple_of(col * TILE, TILE), TILE)]
        moved = lax.dot_general(
            block,
            one_hot_t(cw_ref[pl.ds(col, 1), :]),
            (((1,), (1,)), ((), ())),
            preferred_element_type=jnp.float32,
        ).astype(jnp.bfloat16)
        tile = jnp.dot(perm, moved, preferred_element_type=jnp.float32)
        keep = jnp.full((TILE, TILE), present[slot], jnp.int32) != 0
        out_ref[k] = jnp.where(keep, tile, 0.0).astype(jnp.bfloat16)


def pack_second(src, present, which, children, col_within, row_within):
    n_slots, per_step = SLAB // TILE, 16
    return pl.pallas_call(
        functools.partial(pack_second_kernel, per_step),
        out_shape=jax.ShapeDtypeStruct((n_slots, TILE, TILE), jnp.bfloat16),
        grid_spec=pltpu.PrefetchScalarGridSpec(
            num_scalar_prefetch=3,
            grid=(n_slots // per_step,),
            in_specs=[
                pl.BlockSpec((TILE, children.shape[1]), lambda i, s, p, w: (w[0], 0)),
                pl.BlockSpec(col_within.shape, lambda i, *a: (0, 0)),
                pl.BlockSpec((OWN_TILES, TILE), lambda i, *a: (0, 0)),
            ],
            out_specs=pl.BlockSpec((per_step, TILE, TILE), lambda i, *a: (i, 0, 0)),
        ),
        compiler_params=pltpu.CompilerParams(vmem_limit_bytes=56 * MIB),
        cost_estimate=pl.CostEstimate(
            flops=4 * n_slots * TILE**3,
            bytes_accessed=2 * n_slots * TILE * TILE * 2,
            transcendentals=0,
        ),
    )(src, present, which, children, col_within, row_within)


def sum_kernel(width, counts, bins, seconds, pivots, x_ref, *refs):
    parts, (front_ref, pivot_ref, acc, picked) = refs[: len(counts)], refs[len(counts) :]
    step = pl.program_id(0)
    cols = width * TILE
    per_step = N_DEV // STEPS

    @pl.when(step == 0)
    def _():
        @pl.loop(0, FRONT_TILES)
        def _(i):
            acc[pl.ds(pl.multiple_of(i * TILE, TILE), TILE), :] = jnp.zeros(
                (TILE, cols), jnp.float32
            )

    def add(place, source, index):
        @pl.when(place >= 0)
        def _():
            rows = pl.ds(pl.multiple_of(place * TILE, TILE), TILE)
            for c in range(width):
                acc[rows, c * TILE : (c + 1) * TILE] += source[index, c].astype(jnp.float32)

    for g in range(per_step):
        add(bins[step * per_step + g], x_ref, g)
    at = 0
    for part, count in zip(parts, counts):
        for g in range(count // STEPS):
            add(seconds[at + step * (count // STEPS) + g], part, g)
        at += count

    @pl.when(step == STEPS - 1)
    def _():
        @pl.loop(0, FRONT_TILES)
        def _(i):
            rows = pl.ds(pl.multiple_of(i * TILE, TILE), TILE)
            front_ref[rows, :] = acc[rows, :].astype(jnp.bfloat16)

        @pl.loop(0, TILE)
        def _(j):
            row = pivots[j]
            mine = (row >= 0).astype(jnp.float32)
            value = acc[pl.ds(jnp.maximum(row, 0), 1), :]
            picked[pl.ds(j, 1), :] = value * mine

        pivot_ref[...] = picked[...].astype(jnp.bfloat16)


def sum_chunk(first, width, bins, seconds, pivots, arrived, parts):
    cols = width * TILE
    counts = [p.shape[0] for p in parts]
    return pl.pallas_call(
        functools.partial(sum_kernel, width, counts),
        out_shape=[
            jax.ShapeDtypeStruct((LOCAL_ROWS, cols), jnp.bfloat16),
            jax.ShapeDtypeStruct((TILE, cols), jnp.bfloat16),
        ],
        grid_spec=pltpu.PrefetchScalarGridSpec(
            num_scalar_prefetch=3,
            grid=(STEPS,),
            in_specs=[
                pl.BlockSpec((N_DEV // STEPS, width, TILE, TILE), lambda i, *a: (i, 0, 0, 0))
            ]
            + [
                pl.BlockSpec(
                    (n // STEPS, width, TILE, TILE), lambda i, *a: (i, first // width, 0, 0)
                )
                for n in counts
            ],
            out_specs=[
                pl.BlockSpec((LOCAL_ROWS, cols), lambda i, *a: (0, 0)),
                pl.BlockSpec((TILE, cols), lambda i, *a: (0, 0)),
            ],
            scratch_shapes=[
                pltpu.VMEM((LOCAL_ROWS, cols), jnp.float32),
                pltpu.VMEM((TILE, cols), jnp.float32),
            ],
        ),
        compiler_params=pltpu.CompilerParams(vmem_limit_bytes=56 * MIB),
        cost_estimate=pl.CostEstimate(
            flops=N_DEV * RANKS * TILE * cols,
            bytes_accessed=(N_DEV * RANKS * TILE + LOCAL_ROWS) * cols * 2,
            transcendentals=0,
        ),
    )(bins, seconds, pivots, arrived, *parts)


def accumulate_kernel(width, bins, pivots, x_ref, front_ref, pivot_ref, acc, picked):
    step = pl.program_id(0)
    cols = width * TILE

    @pl.when(step == 0)
    def _():
        @pl.loop(0, FRONT_TILES)
        def _(i):
            acc[pl.ds(pl.multiple_of(i * TILE, TILE), TILE), :] = jnp.zeros(
                (TILE, cols), jnp.float32
            )

    @pl.loop(0, GROUP)
    def _(g):
        for r in range(RANKS):
            place = bins[(step * GROUP + g) * RANKS + r]

            @pl.when(place >= 0)
            def _():
                rows = pl.ds(pl.multiple_of(place * TILE, TILE), TILE)
                for c in range(width):
                    acc[rows, c * TILE : (c + 1) * TILE] += x_ref[g, r, c].astype(
                        jnp.float32
                    )

    @pl.when(step == pl.num_programs(0) - 1)
    def _():
        @pl.loop(0, FRONT_TILES)
        def _(i):
            rows = pl.ds(pl.multiple_of(i * TILE, TILE), TILE)
            front_ref[rows, :] = acc[rows, :].astype(jnp.bfloat16)

        @pl.loop(0, TILE)
        def _(j):
            row = pivots[j]
            mine = (row >= 0).astype(jnp.float32)
            value = acc[pl.ds(jnp.maximum(row, 0), 1), :]
            picked[pl.ds(j, 1), :] = value * mine

        pivot_ref[...] = picked[...].astype(jnp.bfloat16)


def accumulate(width, bins, pivots, arrived):
    cols = width * TILE
    return pl.pallas_call(
        functools.partial(accumulate_kernel, width),
        out_shape=[
            jax.ShapeDtypeStruct((LOCAL_ROWS, cols), jnp.bfloat16),
            jax.ShapeDtypeStruct((TILE, cols), jnp.bfloat16),
        ],
        grid_spec=pltpu.PrefetchScalarGridSpec(
            num_scalar_prefetch=2,
            grid=(N_DEV // GROUP,),
            in_specs=[
                pl.BlockSpec((GROUP, RANKS, width, TILE, TILE), lambda i, *a: (i, 0, 0, 0, 0))
            ],
            out_specs=[
                pl.BlockSpec((LOCAL_ROWS, cols), lambda i, *a: (0, 0)),
                pl.BlockSpec((TILE, cols), lambda i, *a: (0, 0)),
            ],
            scratch_shapes=[
                pltpu.VMEM((LOCAL_ROWS, cols), jnp.float32),
                pltpu.VMEM((TILE, cols), jnp.float32),
            ],
        ),
        compiler_params=pltpu.CompilerParams(vmem_limit_bytes=56 * MIB),
        cost_estimate=pl.CostEstimate(
            flops=N_DEV * RANKS * TILE * cols,
            bytes_accessed=(N_DEV * RANKS * TILE + LOCAL_ROWS) * cols * 2,
            transcendentals=0,
        ),
    )(bins, pivots, arrived)


def update_kernel(n_chunks, my_pcol, *refs):
    fronts, (low_ref, high_ref, pivot_ref, row_ref, linv_ref, uinv_ref, out_ref, upper) = (
        refs[:n_chunks],
        refs[n_chunks:],
    )
    step = pl.program_id(0)

    @pl.when(step == 0)
    def _():
        block = pivot_ref[0].astype(jnp.float32)
        for p in range(1, pivot_ref.shape[0]):
            block = block + pivot_ref[p].astype(jnp.float32)
        upper[...] = jnp.dot(
            linv_ref[...], block.astype(jnp.bfloat16), preferred_element_type=jnp.float32
        ).astype(jnp.bfloat16)

    panel = jnp.concatenate([low_ref[0, 0], high_ref[0, 0]], axis=0)
    lower = (
        jnp.dot(panel, uinv_ref[...], preferred_element_type=jnp.float32)
        .astype(jnp.bfloat16)
        .astype(jnp.float32)
    )
    rows = lax.broadcasted_iota(jnp.int32, (ROW_BLOCK, TILE), 0) + step * ROW_BLOCK
    chosen = jnp.where(rows == row_ref[...], 1.0, 0.0)
    replaced = jnp.max(chosen, axis=1, keepdims=True)
    factor = jnp.where(replaced > 0.0, chosen, -lower).astype(jnp.bfloat16)
    at = 0
    for k in range(n_chunks):
        cols = fronts[k].shape[1]
        product = jnp.dot(
            factor, upper[:, at : at + cols], preferred_element_type=jnp.float32
        )
        result = jnp.where(replaced > 0.0, product, fronts[k][...].astype(jnp.float32) + product)
        out_ref[:, at : at + cols] = result.astype(jnp.bfloat16)
        at += cols

    @pl.when(my_pcol[0] == 0)
    def _():
        out_ref[:, 0:TILE] = lower.astype(jnp.bfloat16)


def update(my_pcol, fronts, panel, pivots, rows, linv, uinv):
    cols, half = SLOTS * TILE, ROW_BLOCK // 2

    def low(i, my_pcol):
        return (i ^ my_pcol[0]) // 4, (i ^ my_pcol[0]) % 4, 0, 0

    def high(i, my_pcol):
        return (i ^ my_pcol[0]) % 4, (i ^ my_pcol[0]) // 4, 0, 0

    whole = lambda *shape: pl.BlockSpec(shape, lambda i, *a: (0,) * len(shape))
    return pl.pallas_call(
        functools.partial(update_kernel, len(fronts)),
        out_shape=jax.ShapeDtypeStruct((LOCAL_ROWS, cols), jnp.bfloat16),
        grid_spec=pltpu.PrefetchScalarGridSpec(
            num_scalar_prefetch=1,
            grid=(LOCAL_ROWS // ROW_BLOCK,),
            in_specs=[
                pl.BlockSpec((ROW_BLOCK, f.shape[1]), lambda i, *a: (i, 0)) for f in fronts
            ]
            + [
                pl.BlockSpec((1, 1, half, TILE), low),
                pl.BlockSpec((1, 1, half, TILE), high),
                whole(*pivots.shape),
                whole(1, TILE),
                whole(TILE, TILE),
                whole(TILE, TILE),
            ],
            out_specs=pl.BlockSpec((ROW_BLOCK, cols), lambda i, *a: (i, 0)),
            scratch_shapes=[pltpu.VMEM((TILE, cols), jnp.bfloat16)],
        ),
        compiler_params=pltpu.CompilerParams(vmem_limit_bytes=56 * MIB),
        cost_estimate=pl.CostEstimate(
            flops=2 * LOCAL_ROWS * TILE * (cols + TILE),
            bytes_accessed=2 * LOCAL_ROWS * cols * 2,
            transcendentals=0,
        ),
    )(my_pcol, *fronts, *panel, pivots, rows, linv, uinv)


def after(value, *others):
    anywhere = pl.BlockSpec(memory_space=pl.ANY)
    return pl.pallas_call(
        lambda *refs: None,
        out_shape=jax.ShapeDtypeStruct(value.shape, value.dtype),
        in_specs=[anywhere] * (1 + len(others)),
        out_specs=anywhere,
        input_output_aliases={0: 0},
    )(value, *others)


def exchange(parts, axes):
    return lax.all_to_all(parts, axes, split_axis=0, concat_axis=0, tiled=True)


def gather_prow(own):
    def shifted(value, by):
        return lax.ppermute(value, "prow", [(p, (p + 2 * by) % N_PROW) for p in range(N_PROW)])

    half = own.shape[0] // 2
    before, after = shifted(own, 1), shifted(own, -1)
    far_low = shifted(before[:half], 1)
    far_high = shifted(after[half:], -1)
    here = [own, before, after, far_low, far_high]
    there = [lax.ppermute(v, "prow", [(p, p ^ 1) for p in range(N_PROW)]) for v in here]
    named = [(0, 2 * half), (0, 2 * half), (0, 2 * half), (0, half), (half, half)]
    shifts = [0, -1, 1, -2, 2]
    places = [
        (flip, shift, begin, count)
        for flip in (0, 1)
        for shift, (begin, count) in zip(shifts, named)
    ]
    return here + there, places


def scatter_panel(panel, my_pcol):
    pieces = panel.reshape(N_PCOL, ROW_BLOCK, TILE)
    piece = pieces[0]
    for q in range(1, N_PCOL):
        got = lax.ppermute(pieces[q], "pcol", [(0, q)])
        piece = jnp.where(my_pcol == q, got, piece)
    return piece


def gather_panel(piece):
    def along(value, stride):
        return jnp.stack(
            [value]
            + [
                lax.ppermute(
                    value, "pcol", [(q, q ^ (stride * i)) for q in range(N_PCOL)]
                )
                for i in range(1, 4)
            ]
        )

    half = ROW_BLOCK // 2
    return along(along(piece[:half], 1), 4), along(along(piece[half:], 4), 1)


def on_device(
    children,
    row_owner,
    row_local,
    row_within,
    column_tile,
    column_within,
    pivot_rows,
    lower_inverse,
    upper_inverse,
):
    my_prow = lax.axis_index("prow")
    my_pcol = lax.axis_index("pcol")
    child = my_prow // (N_PROW // 2)
    col_tile = jnp.take(column_tile, child, axis=0)
    col_within = jnp.take(column_within, child, axis=0)
    n_src = col_tile.shape[0]
    hits = (col_tile[:, None] == jnp.arange(SLAB // TILE, dtype=jnp.int32)[None, :]).astype(
        jnp.int32
    )
    src = jnp.sum(hits * jnp.arange(n_src, dtype=jnp.int32)[:, None], axis=0)
    present = jnp.sum(hits, axis=0)
    order = jnp.arange(OWN_TILES, dtype=jnp.int32)
    earlier = order[None, :] < order[:, None]
    owners = row_owner[:, 0]
    rank = jnp.sum(((owners[:, None] == owners[None, :]) & earlier).astype(jnp.int32), axis=1)

    second = rank == 1
    which = jnp.min(jnp.where(second, order, OWN_TILES - 1)).reshape(1)
    col_line = col_within.reshape(n_src, 1, TILE)
    sent = pack_second(src, present, which, children, col_within, row_within)
    own = exchange(sent.reshape(N_PCOL, SLOTS, TILE, TILE), "pcol")
    parts, places = gather_prow(own)

    code = after(owners * FRONT_TILES + row_local, own)
    codes = jnp.pad(
        code[None, :], ((0, 0), (0, TILE - OWN_TILES))
    )
    codes = lax.all_to_all(
        jnp.broadcast_to(codes[None], (N_DEV, 8, TILE)),
        ("prow", "pcol"),
        split_axis=0,
        concat_axis=0,
        tiled=True,
    )[:, 0, :OWN_TILES]
    mine = codes // FRONT_TILES == my_prow
    nth = jnp.sum((mine[:, None, :] & earlier[None]).astype(jnp.int32), axis=2)
    want = jnp.arange(RANKS, dtype=jnp.int32)[None, :, None]
    is_it = mine[:, None, :] & (nth[:, None, :] == want)
    bins = jnp.max(jnp.where(is_it, (codes % FRONT_TILES)[:, None, :], -1), axis=2)

    owner_of = codes // FRONT_TILES
    again = jnp.sum(
        ((owner_of[:, :, None] == owner_of[:, None, :]) & earlier[None]).astype(jnp.int32), axis=2
    )
    is_second = again == 1
    more = jnp.max(jnp.sum(is_second.astype(jnp.int32), axis=1)) > 1
    seconds = jnp.max(
        jnp.where(is_second & mine, codes % FRONT_TILES, -1), axis=1
    ).reshape(N_PROW, N_PCOL)

    pivot_local = jnp.where(
        pivot_rows // LOCAL_ROWS == my_prow, pivot_rows % LOCAL_ROWS, -1
    ).astype(jnp.int32)
    pcol_line = my_pcol.astype(jnp.int32).reshape(1)
    pivot_line = pivot_local.reshape(1, TILE)
    places = jnp.concatenate(
        [
            jnp.take(seconds, ((my_prow ^ flip) + 2 * shift) % N_PROW, axis=0)[
                begin : begin + count
            ]
            for flip, shift, begin, count in places
        ]
    )

    fronts, picks = {}, {}
    panel, ahead = None, parts[1:3]
    for first, width in CHUNKS:
        sent = pack(
            first, width, 1, src, present, owners, rank, children, col_line, row_within
        )
        if ahead:
            sent = after(sent, *ahead)
        arrived = exchange(sent.reshape(N_DEV, width, TILE, TILE), ("prow", "pcol"))
        fronts[first], picks[first] = sum_chunk(
            first, width, bins[:, 0], places, pivot_local, arrived, parts
        )
        if first == 0:
            piece = scatter_panel(fronts[first][:, :TILE], my_pcol)
            panel = gather_panel(piece)
            ahead = [arrived, *parts]
        else:
            ahead = [arrived, piece]
    fronts = [fronts[k] for k in sorted(fronts)]
    pivots = jnp.concatenate([picks[k] for k in sorted(picks)], axis=1)
    for bit in (1, 2):
        pivots = pivots + lax.ppermute(pivots, "prow", [(p, p ^ bit) for p in range(N_PROW)])
    pivots = jnp.stack(
        [pivots, lax.ppermute(pivots, "prow", [(p, p ^ 4) for p in range(N_PROW)])]
    )

    def narrow():
        return update(
            pcol_line, fronts, panel, pivots, pivot_line, lower_inverse, upper_inverse
        )

    def wide():
        fronts, picks = [], []
        for first, width in WIDE_CHUNKS:
            sent = pack(
                first, width, RANKS, src, present, owners, rank, children, col_line, row_within
            )
            arrived = exchange(
                sent.reshape(N_DEV, RANKS, width, TILE, TILE), ("prow", "pcol")
            )
            front, picked = accumulate(width, bins.reshape(-1), pivot_local, arrived)
            fronts.append(front)
            picks.append(picked)
        panel = gather_panel(scatter_panel(fronts[0][:, :TILE], my_pcol))
        picked = jnp.concatenate(picks, axis=1)
        pivots = exchange(jnp.broadcast_to(picked[None], (N_PROW,) + picked.shape), "prow")
        return update(
            pcol_line, fronts, panel, pivots, pivot_line, lower_inverse, upper_inverse
        )

    return lax.cond(more, wide, narrow)


def solution(mesh):
    placed = (
        P(("prow", "pcol"), None),
        P(("prow", "pcol"), None),
        P(("prow", "pcol")),
        P(("prow", "pcol"), None),
        P(),
        P(),
        P(),
        P(),
        P(),
    )
    return jax.shard_map(
        on_device, mesh=mesh, in_specs=placed, out_specs=P("prow", "pcol"), check_vma=False
    )
```

```python
import functools

import jax
import jax.numpy as jnp
from jax import lax
from jax.experimental import pallas as pl
from jax.experimental.pallas import tpu as pltpu
from jax.sharding import PartitionSpec as P

TILE = 128
FRONT = 90112
SLAB = 8192
N_PROW = 8
N_PCOL = 16
N_DEV = N_PROW * N_PCOL
FRONT_TILES = FRONT // TILE // N_PROW
LOCAL_ROWS = FRONT_TILES * TILE
SLOTS = SLAB // TILE // N_PCOL
OWN_TILES = 8
RANKS = 2
WIDE_CHUNKS = ((0, 1), (1, 1), (2, 2))
CHUNKS = ((0, 1), (2, 2), (1, 1))
GROUP = 8
STEPS = 8
ROW_BLOCK = 704
MIB = 1 << 20


def one_hot_t(index_row):
    slot = lax.broadcasted_iota(jnp.int32, (TILE, TILE), 0)
    return jnp.where(slot == index_row, 1.0, 0.0).astype(jnp.bfloat16)


def pack_kernel(first, ranks, src, present, owner, rank, x_ref, cw_ref, rw_ref, out_ref, perm):
    group, slot = pl.program_id(0), pl.program_id(1)

    @pl.when((group == 0) & (slot == 0))
    def _():
        for t in range(OWN_TILES):
            perm[t] = one_hot_t(rw_ref[t : t + 1, :])

    here = present[group * SLOTS + first + slot]

    @pl.when(here == 0)
    def _():
        out_ref[...] = jnp.zeros_like(out_ref)

    @pl.when(here != 0)
    def _():
        moved = lax.dot_general(
            x_ref[...],
            one_hot_t(cw_ref[0]),
            (((1,), (1,)), ((), ())),
            preferred_element_type=jnp.float32,
        ).astype(jnp.bfloat16)
        for t in reversed(range(OWN_TILES)):
            tile = jnp.dot(
                perm[t], moved[t * TILE : (t + 1) * TILE], preferred_element_type=jnp.float32
            )
            place = rank[t] if ranks == RANKS else 0
            out_ref[owner[t], 0, place, 0] = tile.astype(jnp.bfloat16)


def pack(first, width, ranks, src, present, owner, rank, children, col_within, row_within):
    def source(q, s, src, present, owner, rank):
        return src[q * SLOTS + first + s]

    return pl.pallas_call(
        functools.partial(pack_kernel, first, ranks),
        out_shape=jax.ShapeDtypeStruct(
            (N_PROW, N_PCOL, ranks, width, TILE, TILE), jnp.bfloat16
        ),
        grid_spec=pltpu.PrefetchScalarGridSpec(
            num_scalar_prefetch=4,
            grid=(N_PCOL, width),
            in_specs=[
                pl.BlockSpec((OWN_TILES * TILE, TILE), lambda *a: (0, source(*a))),
                pl.BlockSpec((1, 1, TILE), lambda *a: (source(*a), 0, 0)),
                pl.BlockSpec((OWN_TILES, TILE), lambda *a: (0, 0)),
            ],
            out_specs=pl.BlockSpec(
                (N_PROW, 1, ranks, 1, TILE, TILE), lambda q, s, *a: (0, q, 0, s, 0, 0)
            ),
            scratch_shapes=[pltpu.VMEM((OWN_TILES, TILE, TILE), jnp.bfloat16)],
        ),
        compiler_params=pltpu.CompilerParams(vmem_limit_bytes=56 * MIB),
        cost_estimate=pl.CostEstimate(
            flops=4 * N_PCOL * width * OWN_TILES * TILE**3,
            bytes_accessed=3 * N_PCOL * width * OWN_TILES * TILE * TILE * 2,
            transcendentals=0,
        ),
    )(src, present, owner, rank, children, col_within, row_within)


def pack_second_kernel(per_step, src, present, which, x_ref, cw_ref, rw_ref, out_ref):
    perm = one_hot_t(rw_ref[pl.ds(which[0], 1), :])
    for k in range(per_step):
        slot = pl.program_id(0) * per_step + k
        col = src[slot]
        block = x_ref[:, pl.ds(pl.multiple_of(col * TILE, TILE), TILE)]
        moved = lax.dot_general(
            block,
            one_hot_t(cw_ref[pl.ds(col, 1), :]),
            (((1,), (1,)), ((), ())),
            preferred_element_type=jnp.float32,
        ).astype(jnp.bfloat16)
        tile = jnp.dot(perm, moved, preferred_element_type=jnp.float32)
        keep = jnp.full((TILE, TILE), present[slot], jnp.int32) != 0
        out_ref[k] = jnp.where(keep, tile, 0.0).astype(jnp.bfloat16)


def pack_second(src, present, which, children, col_within, row_within):
    n_slots, per_step = SLAB // TILE, 16
    return pl.pallas_call(
        functools.partial(pack_second_kernel, per_step),
        out_shape=jax.ShapeDtypeStruct((n_slots, TILE, TILE), jnp.bfloat16),
        grid_spec=pltpu.PrefetchScalarGridSpec(
            num_scalar_prefetch=3,
            grid=(n_slots // per_step,),
            in_specs=[
                pl.BlockSpec((TILE, children.shape[1]), lambda i, s, p, w: (w[0], 0)),
                pl.BlockSpec(col_within.shape, lambda i, *a: (0, 0)),
                pl.BlockSpec((OWN_TILES, TILE), lambda i, *a: (0, 0)),
            ],
            out_specs=pl.BlockSpec((per_step, TILE, TILE), lambda i, *a: (i, 0, 0)),
        ),
        compiler_params=pltpu.CompilerParams(vmem_limit_bytes=56 * MIB),
        cost_estimate=pl.CostEstimate(
            flops=4 * n_slots * TILE**3,
            bytes_accessed=2 * n_slots * TILE * TILE * 2,
            transcendentals=0,
        ),
    )(src, present, which, children, col_within, row_within)


def sum_kernel(width, counts, bins, seconds, pivots, x_ref, *refs):
    parts, (front_ref, pivot_ref, acc, picked) = refs[: len(counts)], refs[len(counts) :]
    step = pl.program_id(0)
    cols = width * TILE
    per_step = N_DEV // STEPS

    @pl.when(step == 0)
    def _():
        @pl.loop(0, FRONT_TILES)
        def _(i):
            acc[pl.ds(pl.multiple_of(i * TILE, TILE), TILE), :] = jnp.zeros(
                (TILE, cols), jnp.float32
            )

    def add(place, source, index):
        @pl.when(place >= 0)
        def _():
            rows = pl.ds(pl.multiple_of(place * TILE, TILE), TILE)
            for c in range(width):
                acc[rows, c * TILE : (c + 1) * TILE] += source[index, c].astype(jnp.float32)

    for g in range(per_step):
        add(bins[step * per_step + g], x_ref, g)
    at = 0
    for part, count in zip(parts, counts):
        for g in range(count // STEPS):
            add(seconds[at + step * (count // STEPS) + g], part, g)
        at += count

    @pl.when(step == STEPS - 1)
    def _():
        @pl.loop(0, FRONT_TILES)
        def _(i):
            rows = pl.ds(pl.multiple_of(i * TILE, TILE), TILE)
            front_ref[rows, :] = acc[rows, :].astype(jnp.bfloat16)

        @pl.loop(0, TILE)
        def _(j):
            row = pivots[j]
            mine = (row >= 0).astype(jnp.float32)
            value = acc[pl.ds(jnp.maximum(row, 0), 1), :]
            picked[pl.ds(j, 1), :] = value * mine

        pivot_ref[...] = picked[...].astype(jnp.bfloat16)


def sum_chunk(first, width, bins, seconds, pivots, arrived, parts):
    cols = width * TILE
    counts = [p.shape[0] for p in parts]
    return pl.pallas_call(
        functools.partial(sum_kernel, width, counts),
        out_shape=[
            jax.ShapeDtypeStruct((LOCAL_ROWS, cols), jnp.bfloat16),
            jax.ShapeDtypeStruct((TILE, cols), jnp.bfloat16),
        ],
        grid_spec=pltpu.PrefetchScalarGridSpec(
            num_scalar_prefetch=3,
            grid=(STEPS,),
            in_specs=[
                pl.BlockSpec((N_DEV // STEPS, width, TILE, TILE), lambda i, *a: (i, 0, 0, 0))
            ]
            + [
                pl.BlockSpec(
                    (n // STEPS, width, TILE, TILE), lambda i, *a: (i, first // width, 0, 0)
                )
                for n in counts
            ],
            out_specs=[
                pl.BlockSpec((LOCAL_ROWS, cols), lambda i, *a: (0, 0)),
                pl.BlockSpec((TILE, cols), lambda i, *a: (0, 0)),
            ],
            scratch_shapes=[
                pltpu.VMEM((LOCAL_ROWS, cols), jnp.float32),
                pltpu.VMEM((TILE, cols), jnp.float32),
            ],
        ),
        compiler_params=pltpu.CompilerParams(vmem_limit_bytes=56 * MIB),
        cost_estimate=pl.CostEstimate(
            flops=N_DEV * RANKS * TILE * cols,
            bytes_accessed=(N_DEV * RANKS * TILE + LOCAL_ROWS) * cols * 2,
            transcendentals=0,
        ),
    )(bins, seconds, pivots, arrived, *parts)


def accumulate_kernel(width, bins, pivots, x_ref, front_ref, pivot_ref, acc, picked):
    step = pl.program_id(0)
    cols = width * TILE

    @pl.when(step == 0)
    def _():
        @pl.loop(0, FRONT_TILES)
        def _(i):
            acc[pl.ds(pl.multiple_of(i * TILE, TILE), TILE), :] = jnp.zeros(
                (TILE, cols), jnp.float32
            )

    @pl.loop(0, GROUP)
    def _(g):
        for r in range(RANKS):
            place = bins[(step * GROUP + g) * RANKS + r]

            @pl.when(place >= 0)
            def _():
                rows = pl.ds(pl.multiple_of(place * TILE, TILE), TILE)
                for c in range(width):
                    acc[rows, c * TILE : (c + 1) * TILE] += x_ref[g, r, c].astype(
                        jnp.float32
                    )

    @pl.when(step == pl.num_programs(0) - 1)
    def _():
        @pl.loop(0, FRONT_TILES)
        def _(i):
            rows = pl.ds(pl.multiple_of(i * TILE, TILE), TILE)
            front_ref[rows, :] = acc[rows, :].astype(jnp.bfloat16)

        @pl.loop(0, TILE)
        def _(j):
            row = pivots[j]
            mine = (row >= 0).astype(jnp.float32)
            value = acc[pl.ds(jnp.maximum(row, 0), 1), :]
            picked[pl.ds(j, 1), :] = value * mine

        pivot_ref[...] = picked[...].astype(jnp.bfloat16)


def accumulate(width, bins, pivots, arrived):
    cols = width * TILE
    return pl.pallas_call(
        functools.partial(accumulate_kernel, width),
        out_shape=[
            jax.ShapeDtypeStruct((LOCAL_ROWS, cols), jnp.bfloat16),
            jax.ShapeDtypeStruct((TILE, cols), jnp.bfloat16),
        ],
        grid_spec=pltpu.PrefetchScalarGridSpec(
            num_scalar_prefetch=2,
            grid=(N_DEV // GROUP,),
            in_specs=[
                pl.BlockSpec((GROUP, RANKS, width, TILE, TILE), lambda i, *a: (i, 0, 0, 0, 0))
            ],
            out_specs=[
                pl.BlockSpec((LOCAL_ROWS, cols), lambda i, *a: (0, 0)),
                pl.BlockSpec((TILE, cols), lambda i, *a: (0, 0)),
            ],
            scratch_shapes=[
                pltpu.VMEM((LOCAL_ROWS, cols), jnp.float32),
                pltpu.VMEM((TILE, cols), jnp.float32),
            ],
        ),
        compiler_params=pltpu.CompilerParams(vmem_limit_bytes=56 * MIB),
        cost_estimate=pl.CostEstimate(
            flops=N_DEV * RANKS * TILE * cols,
            bytes_accessed=(N_DEV * RANKS * TILE + LOCAL_ROWS) * cols * 2,
            transcendentals=0,
        ),
    )(bins, pivots, arrived)


def update_kernel(n_chunks, my_pcol, *refs):
    fronts, (low_ref, high_ref, pivot_ref, row_ref, linv_ref, uinv_ref, out_ref, upper) = (
        refs[:n_chunks],
        refs[n_chunks:],
    )
    step = pl.program_id(0)

    @pl.when(step == 0)
    def _():
        block = pivot_ref[0].astype(jnp.float32)
        for p in range(1, pivot_ref.shape[0]):
            block = block + pivot_ref[p].astype(jnp.float32)
        upper[...] = jnp.dot(
            linv_ref[...], block.astype(jnp.bfloat16), preferred_element_type=jnp.float32
        ).astype(jnp.bfloat16)

    panel = jnp.concatenate([low_ref[0, 0], high_ref[0, 0]], axis=0)
    lower = (
        jnp.dot(panel, uinv_ref[...], preferred_element_type=jnp.float32)
        .astype(jnp.bfloat16)
        .astype(jnp.float32)
    )
    rows = lax.broadcasted_iota(jnp.int32, (ROW_BLOCK, TILE), 0) + step * ROW_BLOCK
    chosen = jnp.where(rows == row_ref[...], 1.0, 0.0)
    replaced = jnp.max(chosen, axis=1, keepdims=True)
    factor = jnp.where(replaced > 0.0, chosen, -lower).astype(jnp.bfloat16)
    at = 0
    for k in range(n_chunks):
        cols = fronts[k].shape[1]
        product = jnp.dot(
            factor, upper[:, at : at + cols], preferred_element_type=jnp.float32
        )
        result = jnp.where(replaced > 0.0, product, fronts[k][...].astype(jnp.float32) + product)
        out_ref[:, at : at + cols] = result.astype(jnp.bfloat16)
        at += cols

    @pl.when(my_pcol[0] == 0)
    def _():
        out_ref[:, 0:TILE] = lower.astype(jnp.bfloat16)


def update(my_pcol, fronts, panel, pivots, rows, linv, uinv):
    cols, half = SLOTS * TILE, ROW_BLOCK // 2

    def low(i, my_pcol):
        return (i // 4) ^ (my_pcol[0] % 4), i % 4, 0, 0

    def high(i, my_pcol):
        return (i // 4) ^ (my_pcol[0] // 4), i % 4, 0, 0

    whole = lambda *shape: pl.BlockSpec(shape, lambda i, *a: (0,) * len(shape))
    return pl.pallas_call(
        functools.partial(update_kernel, len(fronts)),
        out_shape=jax.ShapeDtypeStruct((LOCAL_ROWS, cols), jnp.bfloat16),
        grid_spec=pltpu.PrefetchScalarGridSpec(
            num_scalar_prefetch=1,
            grid=(LOCAL_ROWS // ROW_BLOCK,),
            in_specs=[
                pl.BlockSpec((ROW_BLOCK, f.shape[1]), lambda i, *a: (i, 0)) for f in fronts
            ]
            + [
                pl.BlockSpec((1, 1, half, TILE), low),
                pl.BlockSpec((1, 1, half, TILE), high),
                whole(*pivots.shape),
                whole(1, TILE),
                whole(TILE, TILE),
                whole(TILE, TILE),
            ],
            out_specs=pl.BlockSpec((ROW_BLOCK, cols), lambda i, *a: (i, 0)),
            scratch_shapes=[pltpu.VMEM((TILE, cols), jnp.bfloat16)],
        ),
        compiler_params=pltpu.CompilerParams(vmem_limit_bytes=56 * MIB),
        cost_estimate=pl.CostEstimate(
            flops=2 * LOCAL_ROWS * TILE * (cols + TILE),
            bytes_accessed=2 * LOCAL_ROWS * cols * 2,
            transcendentals=0,
        ),
    )(my_pcol, *fronts, *panel, pivots, rows, linv, uinv)


def after(value, *others):
    anywhere = pl.BlockSpec(memory_space=pl.ANY)
    return pl.pallas_call(
        lambda *refs: None,
        out_shape=jax.ShapeDtypeStruct(value.shape, value.dtype),
        in_specs=[anywhere] * (1 + len(others)),
        out_specs=anywhere,
        input_output_aliases={0: 0},
    )(value, *others)


def exchange(parts, axes):
    return lax.all_to_all(parts, axes, split_axis=0, concat_axis=0, tiled=True)


def gather_prow(own, first):
    def shifted(value, by):
        return lax.ppermute(value, "prow", [(p, (p + 2 * by) % N_PROW) for p in range(N_PROW)])

    half = own.shape[0] // 2
    left, right = shifted(own, 1), shifted(own, -1)
    far_low = shifted(after(left[:half], *first), 1)
    far_high = shifted(after(right[half:], *first), -1)
    here = [own, left, right, far_low, far_high]
    there = [lax.ppermute(v, "prow", [(p, p ^ 1) for p in range(N_PROW)]) for v in here]
    named = [(0, 2 * half), (0, 2 * half), (0, 2 * half), (0, half), (half, half)]
    shifts = [0, -1, 1, -2, 2]
    places = [
        (flip, shift, begin, count)
        for flip in (0, 1)
        for shift, (begin, count) in zip(shifts, named)
    ]
    return here + there, places


def from_first(values, mine, pairs):
    result = values[0]
    for i in range(1, 4):
        result = jnp.where(mine == i, lax.ppermute(values[i], "pcol", pairs(i)), result)
    return result


def quarter_panel(panel, my_pcol):
    blocks = panel.reshape(4, 4, ROW_BLOCK, TILE)
    half = ROW_BLOCK // 2
    low = from_first(blocks[:, :, :half], my_pcol % 4, lambda i: [(0, i)])
    high = from_first(blocks[:, :, half:], my_pcol // 4, lambda i: [(0, 4 * i)])
    return low, high


def gather_panel(low, high, my_pcol):
    low = from_first([low] * 4, my_pcol // 4, lambda i: [(k, 4 * i + k) for k in range(4)])
    high = from_first([high] * 4, my_pcol % 4, lambda i: [(4 * k, 4 * k + i) for k in range(4)])

    def along(value, stride):
        moved = [
            lax.ppermute(value, "pcol", [(q, q ^ (stride * i)) for q in range(N_PCOL)])
            for i in range(1, 4)
        ]
        return jnp.stack([value] + moved)

    return along(low, 1), along(high, 4)


def on_device(
    children,
    row_owner,
    row_local,
    row_within,
    column_tile,
    column_within,
    pivot_rows,
    lower_inverse,
    upper_inverse,
):
    my_prow = lax.axis_index("prow")
    my_pcol = lax.axis_index("pcol")
    child = my_prow // (N_PROW // 2)
    col_tile = jnp.take(column_tile, child, axis=0)
    col_within = jnp.take(column_within, child, axis=0)
    n_src = col_tile.shape[0]
    hits = (col_tile[:, None] == jnp.arange(SLAB // TILE, dtype=jnp.int32)[None, :]).astype(
        jnp.int32
    )
    src = jnp.sum(hits * jnp.arange(n_src, dtype=jnp.int32)[:, None], axis=0)
    present = jnp.sum(hits, axis=0)
    order = jnp.arange(OWN_TILES, dtype=jnp.int32)
    earlier = order[None, :] < order[:, None]
    owners = row_owner[:, 0]
    rank = jnp.sum(((owners[:, None] == owners[None, :]) & earlier).astype(jnp.int32), axis=1)

    second = rank == 1
    which = jnp.min(jnp.where(second, order, OWN_TILES - 1)).reshape(1)
    col_line = col_within.reshape(n_src, 1, TILE)
    sent = pack_second(src, present, which, children, col_within, row_within)
    own = exchange(sent.reshape(N_PCOL, SLOTS, TILE, TILE), "pcol")
    packed = {
        first: pack(
            first, width, 1, src, present, owners, rank, children, col_line, row_within
        )
        for first, width in CHUNKS
    }
    parts, places = gather_prow(own, [packed[first] for first, _ in CHUNKS[1:]])

    code = after(owners * FRONT_TILES + row_local, own)
    codes = jnp.pad(
        code[None, :], ((0, 0), (0, TILE - OWN_TILES))
    )
    codes = lax.all_to_all(
        jnp.broadcast_to(codes[None], (N_DEV, 8, TILE)),
        ("prow", "pcol"),
        split_axis=0,
        concat_axis=0,
        tiled=True,
    )[:, 0, :OWN_TILES]
    mine = codes // FRONT_TILES == my_prow
    nth = jnp.sum((mine[:, None, :] & earlier[None]).astype(jnp.int32), axis=2)
    want = jnp.arange(RANKS, dtype=jnp.int32)[None, :, None]
    is_it = mine[:, None, :] & (nth[:, None, :] == want)
    bins = jnp.max(jnp.where(is_it, (codes % FRONT_TILES)[:, None, :], -1), axis=2)

    owner_of = codes // FRONT_TILES
    again = jnp.sum(
        ((owner_of[:, :, None] == owner_of[:, None, :]) & earlier[None]).astype(jnp.int32), axis=2
    )
    is_second = again == 1
    more = jnp.max(jnp.sum(is_second.astype(jnp.int32), axis=1)) > 1
    seconds = jnp.max(
        jnp.where(is_second & mine, codes % FRONT_TILES, -1), axis=1
    ).reshape(N_PROW, N_PCOL)

    pivot_local = jnp.where(
        pivot_rows // LOCAL_ROWS == my_prow, pivot_rows % LOCAL_ROWS, -1
    ).astype(jnp.int32)
    pcol_line = my_pcol.astype(jnp.int32).reshape(1)
    pivot_line = pivot_local.reshape(1, TILE)
    places = jnp.concatenate(
        [
            jnp.take(seconds, ((my_prow ^ flip) + 2 * shift) % N_PROW, axis=0)[
                begin : begin + count
            ]
            for flip, shift, begin, count in places
        ]
    )

    fronts, picks = {}, {}
    panel, ahead = None, [*parts[1:3], codes]
    for first, width in CHUNKS:
        sent = after(packed[first], *ahead)
        arrived = exchange(sent.reshape(N_DEV, width, TILE, TILE), ("prow", "pcol"))
        fronts[first], picks[first] = sum_chunk(
            first, width, bins[:, 0], places, pivot_local, arrived, parts
        )
        if first == 0:
            quarters = quarter_panel(fronts[first][:, :TILE], my_pcol)
            panel = gather_panel(*quarters, my_pcol)
            ahead = quarters
        else:
            ahead = [arrived, *panel]
    fronts = [fronts[k] for k in sorted(fronts)]
    pivots = jnp.concatenate([picks[k] for k in sorted(picks)], axis=1)
    pivots = pivots + lax.ppermute(pivots, "prow", [(p, p ^ 1) for p in range(N_PROW)])
    pivots = jnp.stack(
        [pivots]
        + [
            lax.ppermute(pivots, "prow", [(p, p ^ bit) for p in range(N_PROW)])
            for bit in (2, 4, 6)
        ]
    )

    def narrow():
        return update(
            pcol_line, fronts, panel, pivots, pivot_line, lower_inverse, upper_inverse
        )

    def wide():
        fronts, picks = [], []
        for first, width in WIDE_CHUNKS:
            sent = pack(
                first, width, RANKS, src, present, owners, rank, children, col_line, row_within
            )
            arrived = exchange(
                sent.reshape(N_DEV, RANKS, width, TILE, TILE), ("prow", "pcol")
            )
            front, picked = accumulate(width, bins.reshape(-1), pivot_local, arrived)
            fronts.append(front)
            picks.append(picked)
        panel = gather_panel(*quarter_panel(fronts[0][:, :TILE], my_pcol), my_pcol)
        picked = jnp.concatenate(picks, axis=1)
        pivots = exchange(jnp.broadcast_to(picked[None], (N_PROW,) + picked.shape), "prow")
        return update(
            pcol_line, fronts, panel, pivots, pivot_line, lower_inverse, upper_inverse
        )

    return lax.cond(more, wide, narrow)


def solution(mesh):
    placed = (
        P(("prow", "pcol"), None),
        P(("prow", "pcol"), None),
        P(("prow", "pcol")),
        P(("prow", "pcol"), None),
        P(),
        P(),
        P(),
        P(),
        P(),
    )
    return jax.shard_map(
        on_device, mesh=mesh, in_specs=placed, out_specs=P("prow", "pcol"), check_vma=False
    )
```

```python
import functools

import jax
import jax.numpy as jnp
from jax import lax
from jax.experimental import pallas as pl
from jax.experimental.pallas import tpu as pltpu
from jax.sharding import PartitionSpec as P

TILE = 128
FRONT = 90112
SLAB = 8192
N_PROW = 8
N_PCOL = 16
N_DEV = N_PROW * N_PCOL
FRONT_TILES = FRONT // TILE // N_PROW
LOCAL_ROWS = FRONT_TILES * TILE
SLOTS = SLAB // TILE // N_PCOL
OWN_TILES = 8
RANKS = 2
WIDE_CHUNKS = ((0, 1), (1, 1), (2, 2))
CHUNKS = ((0, 1), (1, 2), (3, 1))
GROUP = 8
STEPS = 8
ROW_BLOCK = 704
MIB = 1 << 20


def one_hot_t(index_row):
    slot = lax.broadcasted_iota(jnp.int32, (TILE, TILE), 0)
    return jnp.where(slot == index_row, 1.0, 0.0).astype(jnp.bfloat16)


def pack_kernel(first, ranks, src, present, owner, rank, x_ref, cw_ref, rw_ref, out_ref, perm):
    group, slot = pl.program_id(0), pl.program_id(1)

    @pl.when((group == 0) & (slot == 0))
    def _():
        for t in range(OWN_TILES):
            perm[t] = one_hot_t(rw_ref[t : t + 1, :])

    here = present[group * SLOTS + first + slot]

    @pl.when(here == 0)
    def _():
        out_ref[...] = jnp.zeros_like(out_ref)

    @pl.when(here != 0)
    def _():
        moved = lax.dot_general(
            x_ref[...],
            one_hot_t(cw_ref[0]),
            (((1,), (1,)), ((), ())),
            preferred_element_type=jnp.float32,
        ).astype(jnp.bfloat16)
        for t in reversed(range(OWN_TILES)):
            tile = jnp.dot(
                perm[t], moved[t * TILE : (t + 1) * TILE], preferred_element_type=jnp.float32
            )
            place = rank[t] if ranks == RANKS else 0
            out_ref[owner[t], 0, place, 0] = tile.astype(jnp.bfloat16)


def pack(first, width, ranks, src, present, owner, rank, children, col_within, row_within):
    def source(q, s, src, present, owner, rank):
        return src[q * SLOTS + first + s]

    return pl.pallas_call(
        functools.partial(pack_kernel, first, ranks),
        out_shape=jax.ShapeDtypeStruct(
            (N_PROW, N_PCOL, ranks, width, TILE, TILE), jnp.bfloat16
        ),
        grid_spec=pltpu.PrefetchScalarGridSpec(
            num_scalar_prefetch=4,
            grid=(N_PCOL, width),
            in_specs=[
                pl.BlockSpec((OWN_TILES * TILE, TILE), lambda *a: (0, source(*a))),
                pl.BlockSpec((1, 1, TILE), lambda *a: (source(*a), 0, 0)),
                pl.BlockSpec((OWN_TILES, TILE), lambda *a: (0, 0)),
            ],
            out_specs=pl.BlockSpec(
                (N_PROW, 1, ranks, 1, TILE, TILE), lambda q, s, *a: (0, q, 0, s, 0, 0)
            ),
            scratch_shapes=[pltpu.VMEM((OWN_TILES, TILE, TILE), jnp.bfloat16)],
        ),
        compiler_params=pltpu.CompilerParams(vmem_limit_bytes=56 * MIB),
        cost_estimate=pl.CostEstimate(
            flops=4 * N_PCOL * width * OWN_TILES * TILE**3,
            bytes_accessed=3 * N_PCOL * width * OWN_TILES * TILE * TILE * 2,
            transcendentals=0,
        ),
    )(src, present, owner, rank, children, col_within, row_within)


def pack_second_kernel(per_step, src, present, which, x_ref, cw_ref, rw_ref, out_ref):
    perm = one_hot_t(rw_ref[pl.ds(which[0], 1), :])
    for k in range(per_step):
        slot = pl.program_id(0) * per_step + k
        col = src[slot]
        block = x_ref[:, pl.ds(pl.multiple_of(col * TILE, TILE), TILE)]
        moved = lax.dot_general(
            block,
            one_hot_t(cw_ref[pl.ds(col, 1), :]),
            (((1,), (1,)), ((), ())),
            preferred_element_type=jnp.float32,
        ).astype(jnp.bfloat16)
        tile = jnp.dot(perm, moved, preferred_element_type=jnp.float32)
        keep = jnp.full((TILE, TILE), present[slot], jnp.int32) != 0
        out_ref[k] = jnp.where(keep, tile, 0.0).astype(jnp.bfloat16)


def pack_second(src, present, which, children, col_within, row_within):
    n_slots, per_step = SLAB // TILE, 16
    return pl.pallas_call(
        functools.partial(pack_second_kernel, per_step),
        out_shape=jax.ShapeDtypeStruct((n_slots, TILE, TILE), jnp.bfloat16),
        grid_spec=pltpu.PrefetchScalarGridSpec(
            num_scalar_prefetch=3,
            grid=(n_slots // per_step,),
            in_specs=[
                pl.BlockSpec((TILE, children.shape[1]), lambda i, s, p, w: (w[0], 0)),
                pl.BlockSpec(col_within.shape, lambda i, *a: (0, 0)),
                pl.BlockSpec((OWN_TILES, TILE), lambda i, *a: (0, 0)),
            ],
            out_specs=pl.BlockSpec((per_step, TILE, TILE), lambda i, *a: (i, 0, 0)),
        ),
        compiler_params=pltpu.CompilerParams(vmem_limit_bytes=56 * MIB),
        cost_estimate=pl.CostEstimate(
            flops=4 * n_slots * TILE**3,
            bytes_accessed=2 * n_slots * TILE * TILE * 2,
            transcendentals=0,
        ),
    )(src, present, which, children, col_within, row_within)


def sum_kernel(width, counts, bins, seconds, pivots, x_ref, *refs):
    parts, (front_ref, pivot_ref, acc, picked) = refs[: len(counts)], refs[len(counts) :]
    step = pl.program_id(0)
    cols = width * TILE
    per_step = N_DEV // STEPS

    @pl.when(step == 0)
    def _():
        @pl.loop(0, FRONT_TILES)
        def _(i):
            acc[pl.ds(pl.multiple_of(i * TILE, TILE), TILE), :] = jnp.zeros(
                (TILE, cols), jnp.float32
            )

    def add(place, source, index):
        @pl.when(place >= 0)
        def _():
            rows = pl.ds(pl.multiple_of(place * TILE, TILE), TILE)
            for c in range(width):
                acc[rows, c * TILE : (c + 1) * TILE] += source[index, c].astype(jnp.float32)

    for g in range(per_step):
        add(bins[step * per_step + g], x_ref, g)
    at = 0
    for part, count in zip(parts, counts):
        for g in range(count // STEPS):
            add(seconds[at + step * (count // STEPS) + g], part, g)
        at += count

    @pl.when(step == STEPS - 1)
    def _():
        @pl.loop(0, FRONT_TILES)
        def _(i):
            rows = pl.ds(pl.multiple_of(i * TILE, TILE), TILE)
            front_ref[rows, :] = acc[rows, :].astype(jnp.bfloat16)

        @pl.loop(0, TILE)
        def _(j):
            row = pivots[j]
            mine = (row >= 0).astype(jnp.float32)
            value = acc[pl.ds(jnp.maximum(row, 0), 1), :]
            picked[pl.ds(j, 1), :] = value * mine

        pivot_ref[...] = picked[...].astype(jnp.bfloat16)


def sum_chunk(first, width, bins, seconds, pivots, arrived, parts):
    cols = width * TILE
    counts = [p.shape[0] for p in parts]
    return pl.pallas_call(
        functools.partial(sum_kernel, width, counts),
        out_shape=[
            jax.ShapeDtypeStruct((LOCAL_ROWS, cols), jnp.bfloat16),
            jax.ShapeDtypeStruct((TILE, cols), jnp.bfloat16),
        ],
        grid_spec=pltpu.PrefetchScalarGridSpec(
            num_scalar_prefetch=3,
            grid=(STEPS,),
            in_specs=[
                pl.BlockSpec((N_DEV // STEPS, width, TILE, TILE), lambda i, *a: (i, 0, 0, 0))
            ]
            + [
                pl.BlockSpec(
                    (n // STEPS, width, TILE, TILE), lambda i, *a: (i, first // width, 0, 0)
                )
                for n in counts
            ],
            out_specs=[
                pl.BlockSpec((LOCAL_ROWS, cols), lambda i, *a: (0, 0)),
                pl.BlockSpec((TILE, cols), lambda i, *a: (0, 0)),
            ],
            scratch_shapes=[
                pltpu.VMEM((LOCAL_ROWS, cols), jnp.float32),
                pltpu.VMEM((TILE, cols), jnp.float32),
            ],
        ),
        compiler_params=pltpu.CompilerParams(vmem_limit_bytes=56 * MIB),
        cost_estimate=pl.CostEstimate(
            flops=N_DEV * RANKS * TILE * cols,
            bytes_accessed=(N_DEV * RANKS * TILE + LOCAL_ROWS) * cols * 2,
            transcendentals=0,
        ),
    )(bins, seconds, pivots, arrived, *parts)


def accumulate_kernel(width, bins, pivots, x_ref, front_ref, pivot_ref, acc, picked):
    step = pl.program_id(0)
    cols = width * TILE

    @pl.when(step == 0)
    def _():
        @pl.loop(0, FRONT_TILES)
        def _(i):
            acc[pl.ds(pl.multiple_of(i * TILE, TILE), TILE), :] = jnp.zeros(
                (TILE, cols), jnp.float32
            )

    @pl.loop(0, GROUP)
    def _(g):
        for r in range(RANKS):
            place = bins[(step * GROUP + g) * RANKS + r]

            @pl.when(place >= 0)
            def _():
                rows = pl.ds(pl.multiple_of(place * TILE, TILE), TILE)
                for c in range(width):
                    acc[rows, c * TILE : (c + 1) * TILE] += x_ref[g, r, c].astype(
                        jnp.float32
                    )

    @pl.when(step == pl.num_programs(0) - 1)
    def _():
        @pl.loop(0, FRONT_TILES)
        def _(i):
            rows = pl.ds(pl.multiple_of(i * TILE, TILE), TILE)
            front_ref[rows, :] = acc[rows, :].astype(jnp.bfloat16)

        @pl.loop(0, TILE)
        def _(j):
            row = pivots[j]
            mine = (row >= 0).astype(jnp.float32)
            value = acc[pl.ds(jnp.maximum(row, 0), 1), :]
            picked[pl.ds(j, 1), :] = value * mine

        pivot_ref[...] = picked[...].astype(jnp.bfloat16)


def accumulate(width, bins, pivots, arrived):
    cols = width * TILE
    return pl.pallas_call(
        functools.partial(accumulate_kernel, width),
        out_shape=[
            jax.ShapeDtypeStruct((LOCAL_ROWS, cols), jnp.bfloat16),
            jax.ShapeDtypeStruct((TILE, cols), jnp.bfloat16),
        ],
        grid_spec=pltpu.PrefetchScalarGridSpec(
            num_scalar_prefetch=2,
            grid=(N_DEV // GROUP,),
            in_specs=[
                pl.BlockSpec((GROUP, RANKS, width, TILE, TILE), lambda i, *a: (i, 0, 0, 0, 0))
            ],
            out_specs=[
                pl.BlockSpec((LOCAL_ROWS, cols), lambda i, *a: (0, 0)),
                pl.BlockSpec((TILE, cols), lambda i, *a: (0, 0)),
            ],
            scratch_shapes=[
                pltpu.VMEM((LOCAL_ROWS, cols), jnp.float32),
                pltpu.VMEM((TILE, cols), jnp.float32),
            ],
        ),
        compiler_params=pltpu.CompilerParams(vmem_limit_bytes=56 * MIB),
        cost_estimate=pl.CostEstimate(
            flops=N_DEV * RANKS * TILE * cols,
            bytes_accessed=(N_DEV * RANKS * TILE + LOCAL_ROWS) * cols * 2,
            transcendentals=0,
        ),
    )(bins, pivots, arrived)


def update_kernel(n_chunks, my_pcol, *refs):
    fronts, (low_ref, high_ref, pivot_ref, row_ref, linv_ref, uinv_ref, out_ref, upper) = (
        refs[:n_chunks],
        refs[n_chunks:],
    )
    step = pl.program_id(0)

    @pl.when(step == 0)
    def _():
        block = pivot_ref[0].astype(jnp.float32)
        for p in range(1, pivot_ref.shape[0]):
            block = block + pivot_ref[p].astype(jnp.float32)
        upper[...] = jnp.dot(
            linv_ref[...], block.astype(jnp.bfloat16), preferred_element_type=jnp.float32
        ).astype(jnp.bfloat16)

    panel = jnp.concatenate([low_ref[0, 0], high_ref[0, 0]], axis=0)
    lower = (
        jnp.dot(panel, uinv_ref[...], preferred_element_type=jnp.float32)
        .astype(jnp.bfloat16)
        .astype(jnp.float32)
    )
    rows = lax.broadcasted_iota(jnp.int32, (ROW_BLOCK, TILE), 0) + step * ROW_BLOCK
    chosen = jnp.where(rows == row_ref[...], 1.0, 0.0)
    replaced = jnp.max(chosen, axis=1, keepdims=True)
    factor = jnp.where(replaced > 0.0, chosen, -lower).astype(jnp.bfloat16)
    at = 0
    for k in range(n_chunks):
        cols = fronts[k].shape[1]
        product = jnp.dot(
            factor, upper[:, at : at + cols], preferred_element_type=jnp.float32
        )
        result = jnp.where(replaced > 0.0, product, fronts[k][...].astype(jnp.float32) + product)
        out_ref[:, at : at + cols] = result.astype(jnp.bfloat16)
        at += cols

    @pl.when(my_pcol[0] == 0)
    def _():
        out_ref[:, 0:TILE] = lower.astype(jnp.bfloat16)


def update(my_pcol, fronts, panel, pivots, rows, linv, uinv):
    cols, half = SLOTS * TILE, ROW_BLOCK // 2

    def low(i, my_pcol):
        return (i // 4) ^ (my_pcol[0] % 4), i % 4, 0, 0

    def high(i, my_pcol):
        return (i // 4) ^ (my_pcol[0] // 4), i % 4, 0, 0

    whole = lambda *shape: pl.BlockSpec(shape, lambda i, *a: (0,) * len(shape))
    return pl.pallas_call(
        functools.partial(update_kernel, len(fronts)),
        out_shape=jax.ShapeDtypeStruct((LOCAL_ROWS, cols), jnp.bfloat16),
        grid_spec=pltpu.PrefetchScalarGridSpec(
            num_scalar_prefetch=1,
            grid=(LOCAL_ROWS // ROW_BLOCK,),
            in_specs=[
                pl.BlockSpec((ROW_BLOCK, f.shape[1]), lambda i, *a: (i, 0)) for f in fronts
            ]
            + [
                pl.BlockSpec((1, 1, half, TILE), low),
                pl.BlockSpec((1, 1, half, TILE), high),
                whole(*pivots.shape),
                whole(1, TILE),
                whole(TILE, TILE),
                whole(TILE, TILE),
            ],
            out_specs=pl.BlockSpec((ROW_BLOCK, cols), lambda i, *a: (i, 0)),
            scratch_shapes=[pltpu.VMEM((TILE, cols), jnp.bfloat16)],
        ),
        compiler_params=pltpu.CompilerParams(vmem_limit_bytes=56 * MIB),
        cost_estimate=pl.CostEstimate(
            flops=2 * LOCAL_ROWS * TILE * (cols + TILE),
            bytes_accessed=2 * LOCAL_ROWS * cols * 2,
            transcendentals=0,
        ),
    )(my_pcol, *fronts, *panel, pivots, rows, linv, uinv)


def after(value, *others):
    anywhere = pl.BlockSpec(memory_space=pl.ANY)
    return pl.pallas_call(
        lambda *refs: None,
        out_shape=jax.ShapeDtypeStruct(value.shape, value.dtype),
        in_specs=[anywhere] * (1 + len(others)),
        out_specs=anywhere,
        input_output_aliases={0: 0},
    )(value, *others)


def exchange(parts, axes):
    return lax.all_to_all(parts, axes, split_axis=0, concat_axis=0, tiled=True)


def shifted(value, by):
    return lax.ppermute(value, "prow", [(p, (p + 2 * by) % N_PROW) for p in range(N_PROW)])


def both_cores(here, named):
    there = [lax.ppermute(v, "prow", [(p, p ^ 1) for p in range(N_PROW)]) for v in here]
    return here + there, [(flip, *name) for flip in (0, 1) for name in named]


def gather_direct(own):
    n = own.shape[0]
    here = [own, shifted(own, 1), shifted(own, -1), shifted(own, 2)]
    return both_cores(here, [(0, 0, n), (-1, 0, n), (1, 0, n), (-2, 0, n)])


def gather_relayed(own):
    n = own.shape[0]
    half = n // 2
    left, right = shifted(own, 1), shifted(own, -1)
    here = [own, left, right, shifted(left[:half], 1), shifted(right[half:], -1)]
    named = [(0, 0, n), (-1, 0, n), (1, 0, n), (-2, 0, half), (-2, half, half)]
    return both_cores(here, named)


def from_first(values, mine, pairs):
    result = values[0]
    for i in range(1, 4):
        result = jnp.where(mine == i, lax.ppermute(values[i], "pcol", pairs(i)), result)
    return result


def quarter_panel(panel, my_pcol):
    blocks = panel.reshape(4, 4, ROW_BLOCK, TILE)
    half = ROW_BLOCK // 2
    low = from_first(blocks[:, :, :half], my_pcol % 4, lambda i: [(0, i)])
    high = from_first(blocks[:, :, half:], my_pcol // 4, lambda i: [(0, 4 * i)])
    return low, high


def spread_quarters(low, high, my_pcol):
    low = from_first([low] * 4, my_pcol // 4, lambda i: [(k, 4 * i + k) for k in range(4)])
    high = from_first([high] * 4, my_pcol % 4, lambda i: [(4 * k, 4 * k + i) for k in range(4)])
    return low, high


def gather_panel(low, high):
    def along(value, stride):
        moved = [
            lax.ppermute(value, "pcol", [(q, q ^ (stride * i)) for q in range(N_PCOL)])
            for i in range(1, 4)
        ]
        return jnp.stack([value] + moved)

    return along(low, 1), along(high, 4)


def on_device(
    children,
    row_owner,
    row_local,
    row_within,
    column_tile,
    column_within,
    pivot_rows,
    lower_inverse,
    upper_inverse,
):
    my_prow = lax.axis_index("prow")
    my_pcol = lax.axis_index("pcol")
    child = my_prow // (N_PROW // 2)
    col_tile = jnp.take(column_tile, child, axis=0)
    col_within = jnp.take(column_within, child, axis=0)
    n_src = col_tile.shape[0]
    hits = (col_tile[:, None] == jnp.arange(SLAB // TILE, dtype=jnp.int32)[None, :]).astype(
        jnp.int32
    )
    src = jnp.sum(hits * jnp.arange(n_src, dtype=jnp.int32)[:, None], axis=0)
    present = jnp.sum(hits, axis=0)
    order = jnp.arange(OWN_TILES, dtype=jnp.int32)
    earlier = order[None, :] < order[:, None]
    owners = row_owner[:, 0]
    rank = jnp.sum(((owners[:, None] == owners[None, :]) & earlier).astype(jnp.int32), axis=1)

    second = rank == 1
    which = jnp.min(jnp.where(second, order, OWN_TILES - 1)).reshape(1)
    col_line = col_within.reshape(n_src, 1, TILE)
    sent = pack_second(src, present, which, children, col_within, row_within)
    own = exchange(sent.reshape(N_PCOL, SLOTS, TILE, TILE), "pcol")
    packed = {
        first: pack(
            first, width, 1, src, present, owners, rank, children, col_line, row_within
        )
        for first, width in CHUNKS
    }
    near_parts, near_places = gather_direct(own[:, :1])
    far_own = after(own[:, 1:], *[packed[first] for first, _ in CHUNKS[1:]])
    far_parts, far_places = gather_relayed(far_own)

    code = after(owners * FRONT_TILES + row_local, own)
    codes = jnp.pad(
        code[None, :], ((0, 0), (0, TILE - OWN_TILES))
    )
    codes = lax.all_to_all(
        jnp.broadcast_to(codes[None], (N_DEV, 8, TILE)),
        ("prow", "pcol"),
        split_axis=0,
        concat_axis=0,
        tiled=True,
    )[:, 0, :OWN_TILES]
    mine = codes // FRONT_TILES == my_prow
    nth = jnp.sum((mine[:, None, :] & earlier[None]).astype(jnp.int32), axis=2)
    want = jnp.arange(RANKS, dtype=jnp.int32)[None, :, None]
    is_it = mine[:, None, :] & (nth[:, None, :] == want)
    bins = jnp.max(jnp.where(is_it, (codes % FRONT_TILES)[:, None, :], -1), axis=2)

    owner_of = codes // FRONT_TILES
    again = jnp.sum(
        ((owner_of[:, :, None] == owner_of[:, None, :]) & earlier[None]).astype(jnp.int32), axis=2
    )
    is_second = again == 1
    more = jnp.max(jnp.sum(is_second.astype(jnp.int32), axis=1)) > 1
    seconds = jnp.max(
        jnp.where(is_second & mine, codes % FRONT_TILES, -1), axis=1
    ).reshape(N_PROW, N_PCOL)

    pivot_local = jnp.where(
        pivot_rows // LOCAL_ROWS == my_prow, pivot_rows % LOCAL_ROWS, -1
    ).astype(jnp.int32)
    pcol_line = my_pcol.astype(jnp.int32).reshape(1)
    pivot_line = pivot_local.reshape(1, TILE)

    def bins_of(places):
        return jnp.concatenate(
            [
                jnp.take(seconds, ((my_prow ^ flip) + 2 * shift) % N_PROW, axis=0)[
                    begin : begin + count
                ]
                for flip, shift, begin, count in places
            ]
        )

    fronts, picks = {}, {}
    panel, ahead = None, [*near_parts[1:4], codes]
    for first, width in CHUNKS:
        sent = after(packed[first], *ahead)
        arrived = exchange(sent.reshape(N_DEV, width, TILE, TILE), ("prow", "pcol"))
        parts, places = (near_parts, near_places) if first == 0 else (far_parts, far_places)
        fronts[first], picks[first] = sum_chunk(
            max(first - 1, 0), width, bins[:, 0], bins_of(places), pivot_local, arrived, parts
        )
        if first == 0:
            quarters = quarter_panel(fronts[first][:, :TILE], my_pcol)
            spread = spread_quarters(*quarters, my_pcol)
            panel = gather_panel(*spread)
            ahead = [*spread, *far_parts[3:5]]
        else:
            ahead = [arrived, *panel]
    fronts = [fronts[k] for k in sorted(fronts)]
    pivots = jnp.concatenate([picks[k] for k in sorted(picks)], axis=1)
    pivots = pivots + lax.ppermute(pivots, "prow", [(p, p ^ 1) for p in range(N_PROW)])
    pivots = jnp.stack(
        [pivots]
        + [
            lax.ppermute(pivots, "prow", [(p, p ^ bit) for p in range(N_PROW)])
            for bit in (2, 4, 6)
        ]
    )

    def narrow():
        return update(
            pcol_line, fronts, panel, pivots, pivot_line, lower_inverse, upper_inverse
        )

    def wide():
        fronts, picks = [], []
        for first, width in WIDE_CHUNKS:
            sent = pack(
                first, width, RANKS, src, present, owners, rank, children, col_line, row_within
            )
            arrived = exchange(
                sent.reshape(N_DEV, RANKS, width, TILE, TILE), ("prow", "pcol")
            )
            front, picked = accumulate(width, bins.reshape(-1), pivot_local, arrived)
            fronts.append(front)
            picks.append(picked)
        quarters = quarter_panel(fronts[0][:, :TILE], my_pcol)
        panel = gather_panel(*spread_quarters(*quarters, my_pcol))
        picked = jnp.concatenate(picks, axis=1)
        pivots = exchange(jnp.broadcast_to(picked[None], (N_PROW,) + picked.shape), "prow")
        return update(
            pcol_line, fronts, panel, pivots, pivot_line, lower_inverse, upper_inverse
        )

    return lax.cond(more, wide, narrow)


def solution(mesh):
    placed = (
        P(("prow", "pcol"), None),
        P(("prow", "pcol"), None),
        P(("prow", "pcol")),
        P(("prow", "pcol"), None),
        P(),
        P(),
        P(),
        P(),
        P(),
    )
    return jax.shard_map(
        on_device, mesh=mesh, in_specs=placed, out_specs=P("prow", "pcol"), check_vma=False
    )
```

```python
import functools

import jax
import jax.numpy as jnp
from jax import lax
from jax.experimental import pallas as pl
from jax.experimental.pallas import tpu as pltpu
from jax.sharding import PartitionSpec as P

TILE = 128
FRONT = 90112
SLAB = 8192
N_PROW = 8
N_PCOL = 16
N_DEV = N_PROW * N_PCOL
FRONT_TILES = FRONT // TILE // N_PROW
LOCAL_ROWS = FRONT_TILES * TILE
SLOTS = SLAB // TILE // N_PCOL
OWN_TILES = 8
RANKS = 2
WIDE_CHUNKS = ((0, 1), (1, 1), (2, 2))
CHUNKS = ((0, 1), (1, 2), (3, 1))
GROUP = 8
STEPS = 8
ROW_BLOCK = 704
MIB = 1 << 20


def one_hot_t(index_row):
    slot = lax.broadcasted_iota(jnp.int32, (TILE, TILE), 0)
    return jnp.where(slot == index_row, 1.0, 0.0).astype(jnp.bfloat16)


def pack_kernel(first, ranks, src, present, owner, rank, x_ref, cw_ref, rw_ref, out_ref, perm):
    group, slot = pl.program_id(0), pl.program_id(1)

    @pl.when((group == 0) & (slot == 0))
    def _():
        for t in range(OWN_TILES):
            perm[t] = one_hot_t(rw_ref[t : t + 1, :])

    here = present[group * SLOTS + first + slot]

    @pl.when(here == 0)
    def _():
        out_ref[...] = jnp.zeros_like(out_ref)

    @pl.when(here != 0)
    def _():
        moved = lax.dot_general(
            x_ref[...],
            one_hot_t(cw_ref[0]),
            (((1,), (1,)), ((), ())),
            preferred_element_type=jnp.float32,
        ).astype(jnp.bfloat16)
        for t in reversed(range(OWN_TILES)):
            tile = jnp.dot(
                perm[t], moved[t * TILE : (t + 1) * TILE], preferred_element_type=jnp.float32
            )
            place = rank[t] if ranks == RANKS else 0
            out_ref[owner[t], 0, place, 0] = tile.astype(jnp.bfloat16)


def pack(first, width, ranks, src, present, owner, rank, children, col_within, row_within):
    def source(q, s, src, present, owner, rank):
        return src[q * SLOTS + first + s]

    return pl.pallas_call(
        functools.partial(pack_kernel, first, ranks),
        out_shape=jax.ShapeDtypeStruct(
            (N_PROW, N_PCOL, ranks, width, TILE, TILE), jnp.bfloat16
        ),
        grid_spec=pltpu.PrefetchScalarGridSpec(
            num_scalar_prefetch=4,
            grid=(N_PCOL, width),
            in_specs=[
                pl.BlockSpec((OWN_TILES * TILE, TILE), lambda *a: (0, source(*a))),
                pl.BlockSpec((1, 1, TILE), lambda *a: (source(*a), 0, 0)),
                pl.BlockSpec((OWN_TILES, TILE), lambda *a: (0, 0)),
            ],
            out_specs=pl.BlockSpec(
                (N_PROW, 1, ranks, 1, TILE, TILE), lambda q, s, *a: (0, q, 0, s, 0, 0)
            ),
            scratch_shapes=[pltpu.VMEM((OWN_TILES, TILE, TILE), jnp.bfloat16)],
        ),
        compiler_params=pltpu.CompilerParams(vmem_limit_bytes=56 * MIB),
        cost_estimate=pl.CostEstimate(
            flops=4 * N_PCOL * width * OWN_TILES * TILE**3,
            bytes_accessed=3 * N_PCOL * width * OWN_TILES * TILE * TILE * 2,
            transcendentals=0,
        ),
    )(src, present, owner, rank, children, col_within, row_within)


def pack_second_kernel(per_step, src, present, which, x_ref, cw_ref, rw_ref, out_ref):
    perm = one_hot_t(rw_ref[pl.ds(which[0], 1), :])
    for k in range(per_step):
        slot = pl.program_id(0) * per_step + k
        col = src[slot]
        block = x_ref[:, pl.ds(pl.multiple_of(col * TILE, TILE), TILE)]
        moved = lax.dot_general(
            block,
            one_hot_t(cw_ref[pl.ds(col, 1), :]),
            (((1,), (1,)), ((), ())),
            preferred_element_type=jnp.float32,
        ).astype(jnp.bfloat16)
        tile = jnp.dot(perm, moved, preferred_element_type=jnp.float32)
        keep = jnp.full((TILE, TILE), present[slot], jnp.int32) != 0
        out_ref[k] = jnp.where(keep, tile, 0.0).astype(jnp.bfloat16)


def pack_second(src, present, which, children, col_within, row_within):
    n_slots, per_step = SLAB // TILE, 16
    return pl.pallas_call(
        functools.partial(pack_second_kernel, per_step),
        out_shape=jax.ShapeDtypeStruct((n_slots, TILE, TILE), jnp.bfloat16),
        grid_spec=pltpu.PrefetchScalarGridSpec(
            num_scalar_prefetch=3,
            grid=(n_slots // per_step,),
            in_specs=[
                pl.BlockSpec((TILE, children.shape[1]), lambda i, s, p, w: (w[0], 0)),
                pl.BlockSpec(col_within.shape, lambda i, *a: (0, 0)),
                pl.BlockSpec((OWN_TILES, TILE), lambda i, *a: (0, 0)),
            ],
            out_specs=pl.BlockSpec((per_step, TILE, TILE), lambda i, *a: (i, 0, 0)),
        ),
        compiler_params=pltpu.CompilerParams(vmem_limit_bytes=56 * MIB),
        cost_estimate=pl.CostEstimate(
            flops=4 * n_slots * TILE**3,
            bytes_accessed=2 * n_slots * TILE * TILE * 2,
            transcendentals=0,
        ),
    )(src, present, which, children, col_within, row_within)


def sum_kernel(width, counts, bins, seconds, pivots, x_ref, *refs):
    parts, (front_ref, pivot_ref, acc, picked) = refs[: len(counts)], refs[len(counts) :]
    step = pl.program_id(0)
    cols = width * TILE
    per_step = N_DEV // STEPS

    @pl.when(step == 0)
    def _():
        @pl.loop(0, FRONT_TILES)
        def _(i):
            acc[pl.ds(pl.multiple_of(i * TILE, TILE), TILE), :] = jnp.zeros(
                (TILE, cols), jnp.float32
            )

    def add(place, source, index):
        @pl.when(place >= 0)
        def _():
            rows = pl.ds(pl.multiple_of(place * TILE, TILE), TILE)
            for c in range(width):
                acc[rows, c * TILE : (c + 1) * TILE] += source[index, c].astype(jnp.float32)

    for g in range(per_step):
        add(bins[step * per_step + g], x_ref, g)
    at = 0
    for part, count in zip(parts, counts):
        for g in range(count // STEPS):
            add(seconds[at + step * (count // STEPS) + g], part, g)
        at += count

    @pl.when(step == STEPS - 1)
    def _():
        @pl.loop(0, FRONT_TILES)
        def _(i):
            rows = pl.ds(pl.multiple_of(i * TILE, TILE), TILE)
            front_ref[rows, :] = acc[rows, :].astype(jnp.bfloat16)

        @pl.loop(0, TILE)
        def _(j):
            row = pivots[j]
            mine = (row >= 0).astype(jnp.float32)
            value = acc[pl.ds(jnp.maximum(row, 0), 1), :]
            picked[pl.ds(j, 1), :] = value * mine

        pivot_ref[...] = picked[...].astype(jnp.bfloat16)


def sum_chunk(first, width, bins, seconds, pivots, arrived, parts):
    cols = width * TILE
    counts = [p.shape[0] for p in parts]
    return pl.pallas_call(
        functools.partial(sum_kernel, width, counts),
        out_shape=[
            jax.ShapeDtypeStruct((LOCAL_ROWS, cols), jnp.bfloat16),
            jax.ShapeDtypeStruct((TILE, cols), jnp.bfloat16),
        ],
        grid_spec=pltpu.PrefetchScalarGridSpec(
            num_scalar_prefetch=3,
            grid=(STEPS,),
            in_specs=[
                pl.BlockSpec((N_DEV // STEPS, width, TILE, TILE), lambda i, *a: (i, 0, 0, 0))
            ]
            + [
                pl.BlockSpec(
                    (n // STEPS, width, TILE, TILE), lambda i, *a: (i, first // width, 0, 0)
                )
                for n in counts
            ],
            out_specs=[
                pl.BlockSpec((LOCAL_ROWS, cols), lambda i, *a: (0, 0)),
                pl.BlockSpec((TILE, cols), lambda i, *a: (0, 0)),
            ],
            scratch_shapes=[
                pltpu.VMEM((LOCAL_ROWS, cols), jnp.float32),
                pltpu.VMEM((TILE, cols), jnp.float32),
            ],
        ),
        compiler_params=pltpu.CompilerParams(vmem_limit_bytes=56 * MIB),
        cost_estimate=pl.CostEstimate(
            flops=N_DEV * RANKS * TILE * cols,
            bytes_accessed=(N_DEV * RANKS * TILE + LOCAL_ROWS) * cols * 2,
            transcendentals=0,
        ),
    )(bins, seconds, pivots, arrived, *parts)


def accumulate_kernel(width, bins, pivots, x_ref, front_ref, pivot_ref, acc, picked):
    step = pl.program_id(0)
    cols = width * TILE

    @pl.when(step == 0)
    def _():
        @pl.loop(0, FRONT_TILES)
        def _(i):
            acc[pl.ds(pl.multiple_of(i * TILE, TILE), TILE), :] = jnp.zeros(
                (TILE, cols), jnp.float32
            )

    @pl.loop(0, GROUP)
    def _(g):
        for r in range(RANKS):
            place = bins[(step * GROUP + g) * RANKS + r]

            @pl.when(place >= 0)
            def _():
                rows = pl.ds(pl.multiple_of(place * TILE, TILE), TILE)
                for c in range(width):
                    acc[rows, c * TILE : (c + 1) * TILE] += x_ref[g, r, c].astype(
                        jnp.float32
                    )

    @pl.when(step == pl.num_programs(0) - 1)
    def _():
        @pl.loop(0, FRONT_TILES)
        def _(i):
            rows = pl.ds(pl.multiple_of(i * TILE, TILE), TILE)
            front_ref[rows, :] = acc[rows, :].astype(jnp.bfloat16)

        @pl.loop(0, TILE)
        def _(j):
            row = pivots[j]
            mine = (row >= 0).astype(jnp.float32)
            value = acc[pl.ds(jnp.maximum(row, 0), 1), :]
            picked[pl.ds(j, 1), :] = value * mine

        pivot_ref[...] = picked[...].astype(jnp.bfloat16)


def accumulate(width, bins, pivots, arrived):
    cols = width * TILE
    return pl.pallas_call(
        functools.partial(accumulate_kernel, width),
        out_shape=[
            jax.ShapeDtypeStruct((LOCAL_ROWS, cols), jnp.bfloat16),
            jax.ShapeDtypeStruct((TILE, cols), jnp.bfloat16),
        ],
        grid_spec=pltpu.PrefetchScalarGridSpec(
            num_scalar_prefetch=2,
            grid=(N_DEV // GROUP,),
            in_specs=[
                pl.BlockSpec((GROUP, RANKS, width, TILE, TILE), lambda i, *a: (i, 0, 0, 0, 0))
            ],
            out_specs=[
                pl.BlockSpec((LOCAL_ROWS, cols), lambda i, *a: (0, 0)),
                pl.BlockSpec((TILE, cols), lambda i, *a: (0, 0)),
            ],
            scratch_shapes=[
                pltpu.VMEM((LOCAL_ROWS, cols), jnp.float32),
                pltpu.VMEM((TILE, cols), jnp.float32),
            ],
        ),
        compiler_params=pltpu.CompilerParams(vmem_limit_bytes=56 * MIB),
        cost_estimate=pl.CostEstimate(
            flops=N_DEV * RANKS * TILE * cols,
            bytes_accessed=(N_DEV * RANKS * TILE + LOCAL_ROWS) * cols * 2,
            transcendentals=0,
        ),
    )(bins, pivots, arrived)


def update_kernel(n_chunks, my_pcol, *refs):
    fronts, (low_ref, high_ref, pivot_ref, row_ref, linv_ref, uinv_ref, out_ref, upper) = (
        refs[:n_chunks],
        refs[n_chunks:],
    )
    step = pl.program_id(0)

    @pl.when(step == 0)
    def _():
        block = pivot_ref[0].astype(jnp.float32)
        for p in range(1, pivot_ref.shape[0]):
            block = block + pivot_ref[p].astype(jnp.float32)
        upper[...] = jnp.dot(
            linv_ref[...], block.astype(jnp.bfloat16), preferred_element_type=jnp.float32
        ).astype(jnp.bfloat16)

    panel = jnp.concatenate([low_ref[0, 0], high_ref[0, 0]], axis=0)
    lower = (
        jnp.dot(panel, uinv_ref[...], preferred_element_type=jnp.float32)
        .astype(jnp.bfloat16)
        .astype(jnp.float32)
    )
    rows = lax.broadcasted_iota(jnp.int32, (ROW_BLOCK, TILE), 0) + step * ROW_BLOCK
    chosen = jnp.where(rows == row_ref[...], 1.0, 0.0)
    replaced = jnp.max(chosen, axis=1, keepdims=True)
    factor = jnp.where(replaced > 0.0, chosen, -lower).astype(jnp.bfloat16)
    at = 0
    for k in range(n_chunks):
        cols = fronts[k].shape[1]
        product = jnp.dot(
            factor, upper[:, at : at + cols], preferred_element_type=jnp.float32
        )
        result = jnp.where(replaced > 0.0, product, fronts[k][...].astype(jnp.float32) + product)
        out_ref[:, at : at + cols] = result.astype(jnp.bfloat16)
        at += cols

    @pl.when(my_pcol[0] == 0)
    def _():
        out_ref[:, 0:TILE] = lower.astype(jnp.bfloat16)


def update(my_pcol, fronts, panel, pivots, rows, linv, uinv):
    cols, half = SLOTS * TILE, ROW_BLOCK // 2

    def low(i, my_pcol):
        return (i // 4) ^ (my_pcol[0] % 4), i % 4, 0, 0

    def high(i, my_pcol):
        return (i // 4) ^ (my_pcol[0] // 4), i % 4, 0, 0

    whole = lambda *shape: pl.BlockSpec(shape, lambda i, *a: (0,) * len(shape))
    return pl.pallas_call(
        functools.partial(update_kernel, len(fronts)),
        out_shape=jax.ShapeDtypeStruct((LOCAL_ROWS, cols), jnp.bfloat16),
        grid_spec=pltpu.PrefetchScalarGridSpec(
            num_scalar_prefetch=1,
            grid=(LOCAL_ROWS // ROW_BLOCK,),
            in_specs=[
                pl.BlockSpec((ROW_BLOCK, f.shape[1]), lambda i, *a: (i, 0)) for f in fronts
            ]
            + [
                pl.BlockSpec((1, 1, half, TILE), low),
                pl.BlockSpec((1, 1, half, TILE), high),
                whole(*pivots.shape),
                whole(1, TILE),
                whole(TILE, TILE),
                whole(TILE, TILE),
            ],
            out_specs=pl.BlockSpec((ROW_BLOCK, cols), lambda i, *a: (i, 0)),
            scratch_shapes=[pltpu.VMEM((TILE, cols), jnp.bfloat16)],
        ),
        compiler_params=pltpu.CompilerParams(vmem_limit_bytes=56 * MIB),
        cost_estimate=pl.CostEstimate(
            flops=2 * LOCAL_ROWS * TILE * (cols + TILE),
            bytes_accessed=2 * LOCAL_ROWS * cols * 2,
            transcendentals=0,
        ),
    )(my_pcol, *fronts, *panel, pivots, rows, linv, uinv)


def after(value, *others):
    anywhere = pl.BlockSpec(memory_space=pl.ANY)
    return pl.pallas_call(
        lambda *refs: None,
        out_shape=jax.ShapeDtypeStruct(value.shape, value.dtype),
        in_specs=[anywhere] * (1 + len(others)),
        out_specs=anywhere,
        input_output_aliases={0: 0},
    )(value, *others)


def exchange(parts, axes):
    return lax.all_to_all(parts, axes, split_axis=0, concat_axis=0, tiled=True)


def shifted(value, by):
    return lax.ppermute(value, "prow", [(p, (p + 2 * by) % N_PROW) for p in range(N_PROW)])


def both_cores(here, named):
    there = [lax.ppermute(v, "prow", [(p, p ^ 1) for p in range(N_PROW)]) for v in here]
    return here + there, [(flip, *name) for flip in (0, 1) for name in named]


def gather_direct(own):
    n = own.shape[0]
    here = [own, shifted(own, 1), shifted(own, -1), shifted(own, 2)]
    return both_cores(here, [(0, 0, n), (-1, 0, n), (1, 0, n), (-2, 0, n)])


def gather_relayed(own):
    n = own.shape[0]
    half = n // 2
    left, right = shifted(own, 1), shifted(own, -1)
    here = [own, left, right, shifted(left[:half], 1), shifted(right[half:], -1)]
    named = [(0, 0, n), (-1, 0, n), (1, 0, n), (-2, 0, half), (-2, half, half)]
    return both_cores(here, named)


def from_first(values, mine, pairs):
    result = values[0]
    for i in range(1, 4):
        result = jnp.where(mine == i, lax.ppermute(values[i], "pcol", pairs(i)), result)
    return result


def quarter_panel(panel, my_pcol):
    blocks = panel.reshape(4, 4, ROW_BLOCK, TILE)
    half = ROW_BLOCK // 2
    low = from_first(blocks[:, :, :half], my_pcol % 4, lambda i: [(0, i)])
    high = from_first(blocks[:, :, half:], my_pcol // 4, lambda i: [(0, 4 * i)])
    return low, high


def spread_quarters(low, high, my_pcol):
    low = from_first([low] * 4, my_pcol // 4, lambda i: [(k, 4 * i + k) for k in range(4)])
    high = from_first([high] * 4, my_pcol % 4, lambda i: [(4 * k, 4 * k + i) for k in range(4)])
    return low, high


def gather_panel(low, high):
    def along(value, stride):
        moved = [
            lax.ppermute(value, "pcol", [(q, q ^ (stride * i)) for q in range(N_PCOL)])
            for i in range(1, 4)
        ]
        return jnp.stack([value] + moved)

    return along(low, 1), along(high, 4)


def on_device(
    children,
    row_owner,
    row_local,
    row_within,
    column_tile,
    column_within,
    pivot_rows,
    lower_inverse,
    upper_inverse,
):
    my_prow = lax.axis_index("prow")
    my_pcol = lax.axis_index("pcol")
    child = my_prow // (N_PROW // 2)
    col_tile = jnp.take(column_tile, child, axis=0)
    col_within = jnp.take(column_within, child, axis=0)
    n_src = col_tile.shape[0]
    hits = (col_tile[:, None] == jnp.arange(SLAB // TILE, dtype=jnp.int32)[None, :]).astype(
        jnp.int32
    )
    src = jnp.sum(hits * jnp.arange(n_src, dtype=jnp.int32)[:, None], axis=0)
    present = jnp.sum(hits, axis=0)
    order = jnp.arange(OWN_TILES, dtype=jnp.int32)
    earlier = order[None, :] < order[:, None]
    owners = row_owner[:, 0]
    rank = jnp.sum(((owners[:, None] == owners[None, :]) & earlier).astype(jnp.int32), axis=1)

    second = rank == 1
    which = jnp.min(jnp.where(second, order, OWN_TILES - 1)).reshape(1)
    col_line = col_within.reshape(n_src, 1, TILE)
    sent = pack_second(src, present, which, children, col_within, row_within)
    own = exchange(sent.reshape(N_PCOL, SLOTS, TILE, TILE), "pcol")
    packed = {
        first: pack(
            first, width, 1, src, present, owners, rank, children, col_line, row_within
        )
        for first, width in CHUNKS
    }
    near_parts, near_places = gather_direct(after(own[:, :1], packed[0]))
    far_own = after(own[:, 1:], *[packed[first] for first, _ in CHUNKS[1:]])
    far_parts, far_places = gather_relayed(far_own)

    code = after(owners * FRONT_TILES + row_local, own, packed[0])
    codes = jnp.pad(
        code[None, :], ((0, 0), (0, TILE - OWN_TILES))
    )
    codes = lax.all_to_all(
        jnp.broadcast_to(codes[None], (N_DEV, 8, TILE)),
        ("prow", "pcol"),
        split_axis=0,
        concat_axis=0,
        tiled=True,
    )[:, 0, :OWN_TILES]
    mine = codes // FRONT_TILES == my_prow
    nth = jnp.sum((mine[:, None, :] & earlier[None]).astype(jnp.int32), axis=2)
    want = jnp.arange(RANKS, dtype=jnp.int32)[None, :, None]
    is_it = mine[:, None, :] & (nth[:, None, :] == want)
    bins = jnp.max(jnp.where(is_it, (codes % FRONT_TILES)[:, None, :], -1), axis=2)

    owner_of = codes // FRONT_TILES
    again = jnp.sum(
        ((owner_of[:, :, None] == owner_of[:, None, :]) & earlier[None]).astype(jnp.int32), axis=2
    )
    is_second = again == 1
    more = jnp.max(jnp.sum(is_second.astype(jnp.int32), axis=1)) > 1
    seconds = jnp.max(
        jnp.where(is_second & mine, codes % FRONT_TILES, -1), axis=1
    ).reshape(N_PROW, N_PCOL)

    pivot_local = jnp.where(
        pivot_rows // LOCAL_ROWS == my_prow, pivot_rows % LOCAL_ROWS, -1
    ).astype(jnp.int32)
    pcol_line = my_pcol.astype(jnp.int32).reshape(1)
    pivot_line = pivot_local.reshape(1, TILE)

    def bins_of(places):
        return jnp.concatenate(
            [
                jnp.take(seconds, ((my_prow ^ flip) + 2 * shift) % N_PROW, axis=0)[
                    begin : begin + count
                ]
                for flip, shift, begin, count in places
            ]
        )

    fronts, picks = {}, {}
    panel, ahead = None, [*near_parts[1:4], codes]
    for first, width in CHUNKS:
        sent = after(packed[first], *ahead)
        arrived = exchange(sent.reshape(N_DEV, width, TILE, TILE), ("prow", "pcol"))
        parts, places = (near_parts, near_places) if first == 0 else (far_parts, far_places)
        fronts[first], picks[first] = sum_chunk(
            max(first - 1, 0), width, bins[:, 0], bins_of(places), pivot_local, arrived, parts
        )
        if first == 0:
            quarters = quarter_panel(fronts[first][:, :TILE], my_pcol)
            spread = spread_quarters(*quarters, my_pcol)
            panel = gather_panel(*spread)
            ahead = [*spread, *far_parts[3:5]]
        else:
            ahead = [arrived, *panel]
    fronts = [fronts[k] for k in sorted(fronts)]
    pivots = jnp.concatenate([picks[k] for k in sorted(picks)], axis=1)
    pivots = pivots + lax.ppermute(pivots, "prow", [(p, p ^ 1) for p in range(N_PROW)])
    pivots = jnp.stack(
        [pivots]
        + [
            lax.ppermute(pivots, "prow", [(p, p ^ bit) for p in range(N_PROW)])
            for bit in (2, 4, 6)
        ]
    )

    def narrow():
        return update(
            pcol_line, fronts, panel, pivots, pivot_line, lower_inverse, upper_inverse
        )

    def wide():
        fronts, picks = [], []
        for first, width in WIDE_CHUNKS:
            sent = pack(
                first, width, RANKS, src, present, owners, rank, children, col_line, row_within
            )
            arrived = exchange(
                sent.reshape(N_DEV, RANKS, width, TILE, TILE), ("prow", "pcol")
            )
            front, picked = accumulate(width, bins.reshape(-1), pivot_local, arrived)
            fronts.append(front)
            picks.append(picked)
        quarters = quarter_panel(fronts[0][:, :TILE], my_pcol)
        panel = gather_panel(*spread_quarters(*quarters, my_pcol))
        picked = jnp.concatenate(picks, axis=1)
        pivots = exchange(jnp.broadcast_to(picked[None], (N_PROW,) + picked.shape), "prow")
        return update(
            pcol_line, fronts, panel, pivots, pivot_line, lower_inverse, upper_inverse
        )

    return lax.cond(more, wide, narrow)


def solution(mesh):
    placed = (
        P(("prow", "pcol"), None),
        P(("prow", "pcol"), None),
        P(("prow", "pcol")),
        P(("prow", "pcol"), None),
        P(),
        P(),
        P(),
        P(),
        P(),
    )
    return jax.shard_map(
        on_device, mesh=mesh, in_specs=placed, out_specs=P("prow", "pcol"), check_vma=False
    )
```
